512 devices in a mesh: dp: 16 (over x, y_lo, core), ctx: 32 (over z, y_hi).
Axes of the slice: x: 4, y: 8 (y_hi: 4, y_lo: 2; y = y_hi * 2 + y_lo), z: 8, core: 2. Of those that a mesh axis runs over, the one named last changes fastest.
Arguments:
- inputs: bfloat16 [16, 8192, 256], P('dp', 'ctx'), may hold values from -6 to 6
- out_grads: bfloat16 [16, 8192, 256], P('dp', 'ctx'), may hold values from -0.015625 to 0.015625
Outputs:
- filter_grad: float32 [8192, 256], P('ctx')
The draws below stay inside these ranges and needn't reach their ends.
All inputs are finite; a program needn't handle non-finite values.
Results may differ from the reference program's by a relative error of at most 0.0095.
Values may be sent and summed in bfloat16 or wider, within the bound.
No kernel may reach another device: no remote copies, remote signals or barrier semaphores. Data moves between devices by JAX's collectives and lax.ppermute only.
A program may use at most 64 MiB of HBM per device.

```python
import math
import jax
import jax.numpy as jnp
from jax import lax

CH = 256
TOK_DEV = 256
TOKENS = 8192
SEQS = 16
N_CTX = 32


def block_scale(key, shape, shards, low, top_value):
    def one(position, blocks):
        heights = jax.random.uniform(jax.random.fold_in(jax.random.fold_in(key, 6), position), (blocks,), jnp.float32, low / len(shards), top_value / len(shards))
        return jnp.repeat(jnp.exp(heights), shape[position] // blocks).reshape((-1,) + (1,) * (len(shape) - position - 1))

    level = one(*shards[0])
    for cut in shards[1:]:
        level = level * one(*cut)
    return level


def scatter_about(key, shape, deviation, limit, pieces=(), held_as=jnp.bfloat16):
    result = jax.random.normal(key, shape, jnp.float32) * deviation
    if len(pieces) > 0:
        result = block_scale(key, shape, pieces, -0.22, 0.18) * result
    return jnp.clip(result, min=-limit, max=limit).astype(held_as)


def setup_inputs(seed: int = 0) -> dict:
    key_list = jax.random.split(jax.random.key(seed), 3)
    return {
        "inputs": scatter_about(key_list[0], (SEQS, TOKENS, CH), 1.0, 6.0, ((0, 16), (1, 32))),
        "out_grads": scatter_about(key_list[1], (SEQS, TOKENS, CH), (TOKENS * SEQS) ** -0.5, 0.015625, ((0, 16), (1, 32))),
    }


def make_tables(blk):
    span = 2 * blk
    freq = jnp.arange(blk, dtype=jnp.int32)[:, None]
    taps = jnp.arange(blk, dtype=jnp.int32)[None, :]
    angle = ((freq * taps) % span).astype(jnp.float32) * (2.0 * math.pi / span)
    signs = (1 - 2 * (taps % 2)).astype(jnp.float32)
    sine_rows = jnp.where(freq == 0, signs, jnp.sin(angle))
    forward = jnp.concatenate([jnp.cos(angle), sine_rows], axis=0).astype(jnp.bfloat16)
    rows = jnp.arange(span, dtype=jnp.int32)[:, None]
    cols = jnp.arange(blk, dtype=jnp.int32)[None, :]
    angle_back = ((rows * cols) % span).astype(jnp.float32) * (2.0 * math.pi / span)
    weight = jnp.where(cols == 0, 1.0, 2.0).astype(jnp.float32) / span
    cos_part = weight * jnp.cos(angle_back)
    row_signs = (1 - 2 * (rows % 2)).astype(jnp.float32) / span
    sin_part = jnp.where(cols == 0, row_signs, -weight * jnp.sin(angle_back))
    inverse = jnp.concatenate([cos_part, sin_part], axis=1)
    return forward, inverse


def pair_product(grad_spec, in_spec, blk):
    left = grad_spec.astype(jnp.float32)
    right = in_spec.astype(jnp.float32)
    cos_a, sin_a = left[..., :blk, :], left[..., blk:, :]
    cos_b, sin_b = right[..., :blk, :], right[..., blk:, :]
    first = (jnp.arange(blk) == 0)[:, None]
    both = sin_a * sin_b
    real = cos_a * cos_b + jnp.where(first, 0.0, both)
    imag = jnp.where(first, both, cos_a * sin_b - sin_a * cos_b)
    return jnp.concatenate([real, imag], axis=-2)


def reference(inputs, out_grads):
    seqs, tokens, chans = inputs.shape
    blk = TOK_DEV
    nblk = N_CTX
    forward, inverse = make_tables(blk)
    blocks_in = inputs.reshape(seqs, nblk, blk, chans).astype(jnp.float32)
    blocks_grad = out_grads.reshape(seqs, nblk, blk, chans).astype(jnp.float32)
    table = forward.astype(jnp.float32)
    in_spec = jnp.einsum('ft,sntc->snfc', table, blocks_in).astype(jnp.bfloat16)
    grad_spec = jnp.einsum('ft,sntc->snfc', table, blocks_grad).astype(jnp.bfloat16)
    padded = jnp.concatenate([jnp.zeros_like(in_spec), in_spec], axis=1)

    def lag_spectrum(lag):
        start = (nblk - lag).astype(jnp.int32)
        moved = lax.dynamic_slice_in_dim(padded, start, nblk, 1)
        return jnp.sum(pair_product(grad_spec, moved, blk), axis=(0, 1))

    sums = lax.map(lag_spectrum, jnp.arange(nblk, dtype=jnp.int32))
    correlation = jnp.einsum('mf,kfc->kmc', inverse, sums, precision=lax.Precision.HIGHEST)
    positive = correlation[:, :blk]
    negative = correlation[:, blk:]
    later = jnp.concatenate([negative[1:], jnp.zeros((1, blk, chans), jnp.float32)], axis=0)
    return (positive + later).reshape(nblk * blk, chans)
```

```python
import itertools
import math

import jax
import jax.numpy as jnp
import ml_dtypes
import numpy as np
from jax import lax
from jax.experimental import pallas as pl
from jax.experimental.pallas import tpu as pltpu
from jax.sharding import PartitionSpec as P

BLK = 256
NBLK = 32
LANES = 128
PLANE = 128
ROWS = 4
XS = 4
SIZES = {"x": 4, "y_lo": 2, "core": 2, "z": 8, "y_hi": 4}
F32 = jnp.float32
BF16 = jnp.bfloat16
LIMIT = 48 * 1024 * 1024


def groups_over(axes):
    rest = [a for a in SIZES if a not in axes]
    groups = []
    for fixed in itertools.product(*[range(SIZES[a]) for a in rest]):
        group = []
        for moving in itertools.product(*[range(SIZES[a]) for a in axes]):
            place = dict(zip(rest, fixed)) | dict(zip(axes, moving))
            flat = 0
            for a in SIZES:
                flat = flat * SIZES[a] + place[a]
            group.append(flat)
        groups.append(group)
    return groups


PLANE_GROUPS = groups_over(("z", "y_hi", "y_lo", "core"))
X_GROUPS = groups_over(("x",))


def exchange(rows, groups):
    return lax.all_to_all(rows, ("dp", "ctx"), 0, 0, axis_index_groups=groups, tiled=True)


def make_tables():
    span = 2 * BLK
    freq = np.arange(BLK)[:, None]
    taps = np.arange(BLK)[None, :]
    angle = (freq * taps % span) * (2.0 * math.pi / span)
    signs = 1.0 - 2.0 * (taps % 2)
    sines = np.where(freq == 0, signs, np.sin(angle))
    forward = np.concatenate([np.cos(angle), sines], axis=0)
    weight = np.where(freq == 0, 1.0, 2.0) / span
    back = np.concatenate([weight * np.cos(angle), np.where(freq == 0, signs / span, -weight * np.sin(angle))], axis=0)
    back = back.astype(np.float32)
    high = back.astype(ml_dtypes.bfloat16)
    low = (back - high.astype(np.float32)).astype(ml_dtypes.bfloat16)
    return forward.T.astype(ml_dtypes.bfloat16), high, low


def dot(a, b):
    return jnp.dot(a, b, preferred_element_type=F32)


def permutation(source_of):
    row = lax.broadcasted_iota(jnp.int32, (BLK, BLK), 0)
    col = lax.broadcasted_iota(jnp.int32, (BLK, BLK), 1)
    return jnp.where(col == source_of(row), 1.0, 0.0).astype(BF16)


def pack_kernel(in_ref, grad_ref, out_ref):
    turned = [jnp.transpose(in_ref[...].astype(F32)).astype(BF16), jnp.transpose(grad_ref[...].astype(F32)).astype(BF16)]
    perm = permutation(lambda m: (m & 7) * 32 + (m >> 3))
    for part in range(4):
        pieces = []
        for a in range(2):
            for c in range(2):
                for th in range(2):
                    start = c * LANES + part * 32
                    pieces.append(turned[a][start : start + 32, th * LANES : (th + 1) * LANES])
        out_ref[part * BLK : (part + 1) * BLK, :] = dot(perm, jnp.concatenate(pieces, axis=0)).astype(BF16)


def correlate_kernel(rows_ref, forward_ref, high_ref, low_ref, out_ref, xc, xs, xd, gc, gs, zed, ybuf):
    def source(m):
        a, th, j8, r, c = m >> 7, (m >> 6) & 1, (m >> 3) & 7, (m >> 1) & 3, m & 1
        return j8 * 32 + r * 8 + a * 4 + c * 2 + th

    perm = permutation(source)
    blocks = [[], []]
    for part in range(4):
        q = dot(perm, rows_ref[part * BLK : (part + 1) * BLK, :]).astype(BF16)
        for a in range(2):
            at = a * 128
            blocks[a].append(jnp.concatenate([q[at : at + 64], q[at + 64 : at + 128]], axis=1))
    first = lax.broadcasted_iota(jnp.int32, (BLK, LANES), 1) == 0
    forward = forward_ref[...]
    spec_in = dot(jnp.concatenate(blocks[0], axis=0), forward).astype(BF16).astype(F32)
    spec_grad = dot(jnp.concatenate(blocks[1], axis=0), forward).astype(BF16).astype(F32)
    for half in range(2):
        up = slice(half * LANES, (half + 1) * LANES)
        down = slice(BLK + half * LANES, BLK + (half + 1) * LANES)
        cos_in, sin_in = spec_in[:, up], spec_in[:, down]
        xc[half] = cos_in
        if half == 0:
            xs[half] = jnp.where(first, 0.0, sin_in)
            xd[half] = jnp.where(first, -sin_in, cos_in)
        else:
            xs[half] = sin_in
            xd[half] = cos_in
        gc[half] = spec_grad[:, up]
        gs[half] = spec_grad[:, down]

    sign = jnp.where(lax.broadcasted_iota(jnp.int32, (8, LANES), 1) % 2 == 0, 1.0, -1.0)
    width = 4

    def one_half(half, carry):
        def at(ref, j):
            return ref[half, j * 8 : (j + 1) * 8, :]

        after_re = jnp.zeros((8, LANES), F32)
        after_im = jnp.zeros((8, LANES), F32)
        for k0 in reversed(range(0, NBLK, width)):
            re = [None] * width
            im = [None] * width
            for i in range(k0, NBLK):
                g_c, g_s = at(gc, i), at(gs, i)
                for kk in range(width):
                    j = i - k0 - kk
                    if j < 0:
                        continue
                    x_c, x_s, x_d = at(xc, j), at(xs, j), at(xd, j)
                    new_re = g_c * x_c + g_s * x_s
                    new_im = g_c * x_s - g_s * x_d
                    re[kk] = new_re if re[kk] is None else re[kk] + new_re
                    im[kk] = new_im if im[kk] is None else im[kk] + new_im
            for kk in reversed(range(width)):
                k = k0 + kk
                for value, after, where in ((re[kk], after_re, 0), (im[kk], after_im, 1)):
                    total = value + sign * after
                    total = total + pltpu.roll(total, 4, 0)
                    total = total + pltpu.roll(total, 2, 0)
                    zed[where * 2 + half, 2 * k : 2 * k + 2, :] = total[0:2]
                after_re, after_im = re[kk], im[kk]
        return carry

    lax.fori_loop(0, 2, one_half, 0)
    z = jnp.concatenate([zed[n] for n in range(4)], axis=1)
    z_high = z.astype(BF16)
    z_low = (z - z_high.astype(F32)).astype(BF16)
    high = high_ref[...]
    y = dot(z_high, high) + (dot(z_low, high) + dot(z_high, low_ref[...]))
    for lh in range(2):
        ybuf[pl.ds(lh, 64, stride=2), :] = y[:, lh * LANES : (lh + 1) * LANES]
    y = ybuf[...].astype(BF16)
    for n in range(XS):
        out_ref[n * LANES : (n + 1) * LANES, :] = y


def total_kernel(parts_ref, out_ref):
    total = parts_ref[0:LANES].astype(F32)
    for n in range(1, XS):
        total = total + parts_ref[n * LANES : (n + 1) * LANES].astype(F32)
    row = lax.broadcasted_iota(jnp.int32, (512, LANES), 0)
    col = lax.broadcasted_iota(jnp.int32, (512, LANES), 1)
    repeat = jnp.where(col == (row >> 4) * 4 + (row & 3), 1.0, 0.0).astype(BF16)
    out_ref[...] = dot(repeat, total.astype(BF16)).astype(BF16)


def unpack_kernel(rows_ref, out_ref):
    perm = permutation(lambda m: (m & 63) * 4 + (m >> 6))
    halves = [dot(perm, rows_ref[part * BLK : (part + 1) * BLK, :]) for part in range(2)]
    for c in range(2):
        for lh in range(2):
            s = c * 2 + lh
            block = jnp.concatenate([h[s * 64 : (s + 1) * 64] for h in halves], axis=0)
            out_ref[lh * LANES : (lh + 1) * LANES, c * LANES : (c + 1) * LANES] = jnp.transpose(block)


def call(kernel, shape, dtype, count, scratch=()):
    return pl.pallas_call(
        kernel,
        out_shape=jax.ShapeDtypeStruct(shape, dtype),
        in_specs=[pl.BlockSpec(memory_space=pltpu.VMEM)] * count,
        out_specs=pl.BlockSpec(memory_space=pltpu.VMEM),
        scratch_shapes=list(scratch),
        compiler_params=pltpu.CompilerParams(vmem_limit_bytes=LIMIT),
    )


def on_device(inputs, out_grads):
    forward, high, low = make_tables()
    rows = call(pack_kernel, (1024, LANES), BF16, 2)(inputs[0], out_grads[0])
    rows = exchange(rows, PLANE_GROUPS)
    spec = pltpu.VMEM((2, BLK, LANES), F32)
    scratch = [spec] * 5 + [pltpu.VMEM((4, 64, LANES), F32), pltpu.VMEM((LANES, LANES), F32)]
    parts = call(correlate_kernel, (XS * LANES, LANES), BF16, 4, scratch)(rows, forward, high, low)
    parts = exchange(parts, X_GROUPS)
    rows = call(total_kernel, (512, LANES), BF16, 1)(parts)
    rows = exchange(rows, PLANE_GROUPS)
    return call(unpack_kernel, (BLK, BLK), F32, 1)(rows)


def solution(mesh):
    in_specs = (P("dp", "ctx", None), P("dp", "ctx", None))
    out_specs = P("ctx", None)
    return jax.shard_map(on_device, mesh=mesh, in_specs=in_specs, out_specs=out_specs, check_vma=False)
```

```python
import itertools
import math

import jax
import jax.numpy as jnp
import ml_dtypes
import numpy as np
from jax import lax
from jax.experimental import pallas as pl
from jax.experimental.pallas import tpu as pltpu
from jax.sharding import PartitionSpec as P

BLK = 256
NBLK = 32
LANES = 128
SIZES = {"x": 4, "y_lo": 2, "core": 2, "z": 8, "y_hi": 4}
F32 = jnp.float32
BF16 = jnp.bfloat16
LIMIT = 48 * 1024 * 1024


def groups_over(axes):
    rest = [a for a in SIZES if a not in axes]
    groups = []
    for fixed in itertools.product(*[range(SIZES[a]) for a in rest]):
        group = []
        for moving in itertools.product(*[range(SIZES[a]) for a in axes]):
            place = dict(zip(rest, fixed)) | dict(zip(axes, moving))
            flat = 0
            for a in SIZES:
                flat = flat * SIZES[a] + place[a]
            group.append(flat)
        groups.append(group)
    return groups


HALF_GROUPS = groups_over(("z", "y_hi", "y_lo"))
SUM_GROUPS = groups_over(("x", "core"))
PLANE_GROUPS = groups_over(("z", "y_hi", "y_lo", "core"))


def exchange(rows, groups):
    return lax.all_to_all(rows, ("dp", "ctx"), 0, 0, axis_index_groups=groups, tiled=True)


def make_tables():
    span = 2 * BLK
    freq = np.arange(BLK)[:, None]
    taps = np.arange(BLK)[None, :]
    angle = (freq * taps % span) * (2.0 * math.pi / span)
    signs = 1.0 - 2.0 * (taps % 2)
    sines = np.where(freq == 0, signs, np.sin(angle))
    forward = np.concatenate([np.cos(angle), sines], axis=0)
    weight = np.where(freq == 0, 1.0, 2.0) / span
    back = np.concatenate([weight * np.cos(angle), np.where(freq == 0, signs / span, -weight * np.sin(angle))], axis=0)
    back = back.astype(np.float32)
    high = back.astype(ml_dtypes.bfloat16)
    low = (back - high.astype(np.float32)).astype(ml_dtypes.bfloat16)
    return forward.T.astype(ml_dtypes.bfloat16), high, low


def dot(a, b):
    return jnp.dot(a, b, preferred_element_type=F32)


def permutation(source_of):
    row = lax.broadcasted_iota(jnp.int32, (BLK, BLK), 0)
    col = lax.broadcasted_iota(jnp.int32, (BLK, BLK), 1)
    return jnp.where(col == source_of(row), 1.0, 0.0).astype(BF16)


def pack_kernel(in_hbm, grad_hbm, out_ref, held, sems):
    copies = [pltpu.make_async_copy(ref, held.at[a], sems.at[a]) for a, ref in enumerate((in_hbm, grad_hbm))]
    for copy in copies:
        copy.start()
    perm = permutation(lambda m: (m & 15) * 16 + (m >> 4))
    turned = []
    for a in range(2):
        copies[a].wait()
        turned.append(jnp.transpose(held[a].astype(F32)).astype(BF16))
    for part in range(4):
        pieces = []
        for a in range(2):
            for c in range(4):
                for th in range(2):
                    start = c * 64 + part * 16
                    pieces.append(turned[a][start : start + 16, th * LANES : (th + 1) * LANES])
        out_ref[part * BLK : (part + 1) * BLK, :] = dot(perm, jnp.concatenate(pieces, axis=0)).astype(BF16)


def correlate_kernel(rows_ref, forward_ref, high_ref, low_ref, out_ref, xa, xb, xc, ga, gb, gc, zed, ybuf):
    def source(m):
        a, th, j8, r, c = m >> 7, (m >> 6) & 1, (m >> 3) & 7, (m >> 2) & 1, m & 3
        return j8 * 32 + r * 16 + a * 8 + c * 2 + th

    perm = permutation(source)
    blocks = [[], []]
    for part in range(4):
        q = dot(perm, rows_ref[part * BLK : (part + 1) * BLK, :]).astype(BF16)
        for a in range(2):
            at = a * 128
            blocks[a].append(jnp.concatenate([q[at : at + 64], q[at + 64 : at + 128]], axis=1))
    first = lax.broadcasted_iota(jnp.int32, (BLK, LANES), 1) == 0
    forward = forward_ref[...]
    spec_in = dot(jnp.concatenate(blocks[0], axis=0), forward).astype(BF16).astype(F32)
    spec_grad = dot(jnp.concatenate(blocks[1], axis=0), forward).astype(BF16).astype(F32)
    for half in range(2):
        up = slice(half * LANES, (half + 1) * LANES)
        down = slice(BLK + half * LANES, BLK + (half + 1) * LANES)
        cos_in, sin_in = spec_in[:, up], spec_in[:, down]
        cos_grad, sin_grad = spec_grad[:, up], spec_grad[:, down]
        x_a, x_b, x_c = cos_in + sin_in, sin_in, cos_in
        g_a, g_b, g_c = cos_grad, cos_grad - sin_grad, cos_grad + sin_grad
        if half == 0:
            x_a = jnp.where(first, 0.0, x_a)
            x_b = jnp.where(first, -cos_in, x_b)
            x_c = jnp.where(first, -sin_in, x_c)
            g_b = jnp.where(first, cos_grad, g_b)
            g_c = jnp.where(first, sin_grad, g_c)
        for ref, value in ((xa, x_a), (xb, x_b), (xc, x_c), (ga, g_a), (gb, g_b), (gc, g_c)):
            ref[half] = value

    sign = jnp.where(lax.broadcasted_iota(jnp.int32, (8, LANES), 1) % 2 == 0, 1.0, -1.0)
    width = 4

    def one_half(half, carry):
        def at(ref, j):
            return ref[half, j * 8 : (j + 1) * 8, :]

        after = [jnp.zeros((8, LANES), F32)] * 2
        for k0 in reversed(range(0, NBLK, width)):
            sums = [[None] * width for _ in range(3)]
            for i in range(k0, NBLK):
                grads = [at(ref, i) for ref in (ga, gb, gc)]
                for kk in range(width):
                    j = i - k0 - kk
                    if j < 0:
                        continue
                    for n, ref in enumerate((xa, xb, xc)):
                        product = grads[n] * at(ref, j)
                        sums[n][kk] = product if sums[n][kk] is None else sums[n][kk] + product
            for kk in reversed(range(width)):
                k = k0 + kk
                now = [sums[0][kk] - sums[1][kk], sums[0][kk] - sums[2][kk]]
                for part in range(2):
                    total = now[part] + sign * after[part]
                    total = total + pltpu.roll(total, 4, 0)
                    for core in range(2):
                        zed[part * 2 + half, core * 64 + 2 * k : core * 64 + 2 * k + 2, :] = total[2 * core : 2 * core + 2]
                after = now
        return carry

    lax.fori_loop(0, 2, one_half, 0)
    z = jnp.concatenate([zed[n] for n in range(4)], axis=1)
    z_high = z.astype(BF16)
    z_low = (z - z_high.astype(F32)).astype(BF16)
    high = high_ref[...]
    y = dot(z_high, high) + (dot(z_low, high) + dot(z_high, low_ref[...]))
    for lh in range(2):
        ybuf[pl.ds(lh, LANES, stride=2), :] = y[:, lh * LANES : (lh + 1) * LANES]
    y = ybuf[...].astype(BF16)
    for x in range(4):
        out_ref[x * BLK : (x + 1) * BLK, :] = y


def total_kernel(parts_ref, out_ref):
    total = parts_ref[0:LANES].astype(F32)
    for n in range(1, 8):
        total = total + parts_ref[n * LANES : (n + 1) * LANES].astype(F32)
    row = lax.broadcasted_iota(jnp.int32, (512, LANES), 0)
    col = lax.broadcasted_iota(jnp.int32, (512, LANES), 1)
    repeat = jnp.where(col == (row >> 4) * 4 + (row & 3), 1.0, 0.0).astype(BF16)
    out_ref[...] = dot(repeat, total.astype(BF16)).astype(BF16)


def unpack_kernel(rows_ref, out_hbm, held, sems):
    def source(m):
        lh, core, c, p = m >> 7, (m >> 6) & 1, (m >> 5) & 1, m & 31
        return (p * 2 + core) * 4 + c * 2 + lh

    perm = permutation(source)
    halves = [dot(perm, rows_ref[part * BLK : (part + 1) * BLK, :]) for part in range(2)]
    copies = []
    for lh in range(2):
        rows = slice(lh * LANES, (lh + 1) * LANES)
        for core in range(2):
            at = lh * 128 + core * 64
            block = jnp.concatenate([halves[part][at + c * 32 : at + c * 32 + 32] for c in range(2) for part in range(2)], axis=0)
            held[rows, core * LANES : (core + 1) * LANES] = jnp.transpose(block)
        copies.append(pltpu.make_async_copy(held.at[rows], out_hbm.at[rows], sems.at[lh]))
        copies[-1].start()
    for copy in copies:
        copy.wait()


def call(kernel, shape, dtype, ins, out, scratch=()):
    return pl.pallas_call(
        kernel,
        out_shape=jax.ShapeDtypeStruct(shape, dtype),
        in_specs=[pl.BlockSpec(memory_space=space) for space in ins],
        out_specs=pl.BlockSpec(memory_space=out),
        scratch_shapes=list(scratch),
        compiler_params=pltpu.CompilerParams(vmem_limit_bytes=LIMIT),
    )


VMEM, HBM = pltpu.VMEM, pltpu.HBM
TWO_SEMS = pltpu.SemaphoreType.DMA((2,))
PACK = call(pack_kernel, (1024, LANES), BF16, [HBM] * 2, VMEM, [VMEM((2, BLK, BLK), BF16), TWO_SEMS])
CORRELATE = call(
    correlate_kernel,
    (1024, LANES),
    BF16,
    [VMEM] * 4,
    VMEM,
    [VMEM((2, BLK, LANES), F32)] * 6 + [VMEM((4, LANES, LANES), F32), VMEM((BLK, LANES), F32)],
)
TOTAL = call(total_kernel, (512, LANES), BF16, [VMEM], VMEM)
UNPACK = call(unpack_kernel, (BLK, BLK), F32, [VMEM], HBM, [VMEM((BLK, BLK), F32), TWO_SEMS])


def on_device(inputs, out_grads):
    rows = PACK(*[pltpu.with_memory_space_constraint(a[0], HBM) for a in (inputs, out_grads)])
    rows = exchange(rows, HALF_GROUPS)
    parts = CORRELATE(rows, *make_tables())
    parts = exchange(parts, SUM_GROUPS)
    rows = TOTAL(parts)
    rows = exchange(rows, PLANE_GROUPS)
    return UNPACK(rows)


def solution(mesh):
    in_specs = (P("dp", "ctx", None), P("dp", "ctx", None))
    out_specs = P("ctx", None)
    return jax.shard_map(on_device, mesh=mesh, in_specs=in_specs, out_specs=out_specs, check_vma=False)
```

```python
import itertools
import math

import jax
import jax.numpy as jnp
import ml_dtypes
import numpy as np
from jax import lax
from jax.experimental import pallas as pl
from jax.experimental.pallas import tpu as pltpu
from jax.sharding import PartitionSpec as P

BLK = 256
NBLK = 32
LANES = 128
SIZES = {"x": 4, "y_lo": 2, "core": 2, "z": 8, "y_hi": 4}
F32 = jnp.float32
BF16 = jnp.bfloat16
LIMIT = 48 * 1024 * 1024


FIRST = {"x": 2, "y_lo": 0, "core": 0, "z": 6, "y_hi": 2}


def turned_range(axis):
    return [(n + FIRST[axis]) % SIZES[axis] for n in range(SIZES[axis])]


def groups_over(axes):
    rest = [a for a in SIZES if a not in axes]
    groups = []
    for fixed in itertools.product(*[range(SIZES[a]) for a in rest]):
        group = []
        for moving in itertools.product(*[turned_range(a) for a in axes]):
            place = dict(zip(rest, fixed)) | dict(zip(axes, moving))
            flat = 0
            for a in SIZES:
                flat = flat * SIZES[a] + place[a]
            group.append(flat)
        groups.append(group)
    return groups


SLOT = [0] * NBLK
for place, (z, y) in enumerate(itertools.product(turned_range("z"), turned_range("y_hi"))):
    SLOT[z * SIZES["y_hi"] + y] = place

HALF_GROUPS = groups_over(("z", "y_hi", "y_lo"))
SUM_GROUPS = groups_over(("x", "core"))
PLANE_GROUPS = groups_over(("z", "y_hi", "y_lo", "core"))


def exchange(rows, groups):
    return lax.all_to_all(rows, ("dp", "ctx"), 0, 0, axis_index_groups=groups, tiled=True)


def make_tables():
    span = 2 * BLK
    freq = np.arange(BLK)[:, None]
    taps = np.arange(BLK)[None, :]
    angle = (freq * taps % span) * (2.0 * math.pi / span)
    signs = 1.0 - 2.0 * (taps % 2)
    sines = np.where(freq == 0, signs, np.sin(angle))
    forward = np.concatenate([np.cos(angle), sines], axis=0)
    weight = np.where(freq == 0, 1.0, 2.0) / span
    back = np.concatenate([weight * np.cos(angle), np.where(freq == 0, signs / span, -weight * np.sin(angle))], axis=0)
    back = back.astype(np.float32)
    high = back.astype(ml_dtypes.bfloat16)
    low = (back - high.astype(np.float32)).astype(ml_dtypes.bfloat16)
    return forward.T.astype(ml_dtypes.bfloat16), high, low


def dot(a, b):
    return jnp.dot(a, b, preferred_element_type=F32)


def permutation(source_of):
    row = lax.broadcasted_iota(jnp.int32, (BLK, BLK), 0)
    col = lax.broadcasted_iota(jnp.int32, (BLK, BLK), 1)
    return jnp.where(col == source_of(row), 1.0, 0.0).astype(BF16)


def pack_kernel(in_hbm, grad_hbm, out_ref, held, sems):
    copies = [pltpu.make_async_copy(ref, held.at[a], sems.at[a]) for a, ref in enumerate((in_hbm, grad_hbm))]
    for copy in copies:
        copy.start()
    perm = permutation(lambda m: (m & 15) * 16 + (m >> 4))
    turned = []
    for a in range(2):
        copies[a].wait()
        turned.append(jnp.transpose(held[a].astype(F32)).astype(BF16))
    for part in range(4):
        pieces = []
        for a in range(2):
            for c in range(4):
                for th in range(2):
                    start = c * 64 + part * 16
                    pieces.append(turned[a][start : start + 16, th * LANES : (th + 1) * LANES])
        out_ref[part * BLK : (part + 1) * BLK, :] = dot(perm, jnp.concatenate(pieces, axis=0)).astype(BF16)


def correlate_kernel(rows_ref, forward_ref, high_ref, low_ref, out_ref, xa, xb, xc, ga, gb, gc, zed, ybuf):
    def source(m):
        a, th, j8, r, c = m >> 7, (m >> 6) & 1, (m >> 3) & 7, (m >> 2) & 1, m & 3
        return j8 * 32 + r * 16 + a * 8 + c * 2 + th

    perm = permutation(source)
    blocks = [[], []]
    for part in range(4):
        q = dot(perm, rows_ref[part * BLK : (part + 1) * BLK, :]).astype(BF16)
        for a in range(2):
            at = a * 128
            blocks[a].append(jnp.concatenate([q[at : at + 64], q[at + 64 : at + 128]], axis=1))
    first = lax.broadcasted_iota(jnp.int32, (BLK, LANES), 1) == 0
    forward = forward_ref[...]
    spec_in = dot(jnp.concatenate(blocks[0], axis=0), forward).astype(BF16).astype(F32)
    spec_grad = dot(jnp.concatenate(blocks[1], axis=0), forward).astype(BF16).astype(F32)
    for half in range(2):
        up = slice(half * LANES, (half + 1) * LANES)
        down = slice(BLK + half * LANES, BLK + (half + 1) * LANES)
        cos_in, sin_in = spec_in[:, up], spec_in[:, down]
        cos_grad, sin_grad = spec_grad[:, up], spec_grad[:, down]
        x_a, x_b, x_c = cos_in + sin_in, sin_in, cos_in
        g_a, g_b, g_c = cos_grad, cos_grad - sin_grad, cos_grad + sin_grad
        if half == 0:
            x_a = jnp.where(first, 0.0, x_a)
            x_b = jnp.where(first, -cos_in, x_b)
            x_c = jnp.where(first, -sin_in, x_c)
            g_b = jnp.where(first, cos_grad, g_b)
            g_c = jnp.where(first, sin_grad, g_c)
        for ref, value in ((xa, x_a), (xb, x_b), (xc, x_c), (ga, g_a), (gb, g_b), (gc, g_c)):
            ref[half] = value

    sign = jnp.where(lax.broadcasted_iota(jnp.int32, (8, LANES), 1) % 2 == 0, 1.0, -1.0)
    width = 4

    for half in range(2):
        def at(ref, j):
            return ref[half, SLOT[j] * 8 : (SLOT[j] + 1) * 8, :]

        after = [jnp.zeros((8, LANES), F32)] * 2
        for k0 in reversed(range(0, NBLK, width)):
            sums = [[None] * width for _ in range(3)]
            for i in range(k0, NBLK):
                grads = [at(ref, i) for ref in (ga, gb, gc)]
                for kk in range(width):
                    j = i - k0 - kk
                    if j < 0:
                        continue
                    for n, ref in enumerate((xa, xb, xc)):
                        product = grads[n] * at(ref, j)
                        sums[n][kk] = product if sums[n][kk] is None else sums[n][kk] + product
            for kk in reversed(range(width)):
                k = k0 + kk
                now = [sums[0][kk] - sums[1][kk], sums[0][kk] - sums[2][kk]]
                for part in range(2):
                    total = now[part] + sign * after[part]
                    total = total + pltpu.roll(total, 4, 0)
                    for core in range(2):
                        at_row = core * 64 + 2 * SLOT[k]
                        zed[part * 2 + half, at_row : at_row + 2, :] = total[2 * core : 2 * core + 2]
                after = now
    z = jnp.concatenate([zed[n] for n in range(4)], axis=1)
    z_high = z.astype(BF16)
    z_low = (z - z_high.astype(F32)).astype(BF16)
    high = high_ref[...]
    y = dot(z_high, high) + (dot(z_low, high) + dot(z_high, low_ref[...]))
    for lh in range(2):
        ybuf[pl.ds(lh, LANES, stride=2), :] = y[:, lh * LANES : (lh + 1) * LANES]
    y = ybuf[...].astype(BF16)
    for x in range(4):
        out_ref[x * BLK : (x + 1) * BLK, :] = y


def total_kernel(parts_ref, out_ref):
    total = parts_ref[0:LANES].astype(F32)
    for n in range(1, 8):
        total = total + parts_ref[n * LANES : (n + 1) * LANES].astype(F32)
    row = lax.broadcasted_iota(jnp.int32, (512, LANES), 0)
    col = lax.broadcasted_iota(jnp.int32, (512, LANES), 1)
    repeat = jnp.where(col == (row >> 4) * 4 + (row & 3), 1.0, 0.0).astype(BF16)
    out_ref[...] = dot(repeat, total.astype(BF16)).astype(BF16)


def unpack_kernel(rows_ref, out_hbm, held, sems):
    def source(m):
        lh, core, c, p = m >> 7, (m >> 6) & 1, (m >> 5) & 1, m & 31
        return (p * 2 + core) * 4 + c * 2 + lh

    perm = permutation(source)
    halves = [dot(perm, rows_ref[part * BLK : (part + 1) * BLK, :]) for part in range(2)]
    copies = []
    for lh in range(2):
        rows = slice(lh * LANES, (lh + 1) * LANES)
        for core in range(2):
            at = lh * 128 + core * 64
            block = jnp.concatenate([halves[part][at + c * 32 : at + c * 32 + 32] for c in range(2) for part in range(2)], axis=0)
            held[rows, core * LANES : (core + 1) * LANES] = jnp.transpose(block)
        copies.append(pltpu.make_async_copy(held.at[rows], out_hbm.at[rows], sems.at[lh]))
        copies[-1].start()
    for copy in copies:
        copy.wait()


def call(kernel, shape, dtype, ins, out, scratch=()):
    return pl.pallas_call(
        kernel,
        out_shape=jax.ShapeDtypeStruct(shape, dtype),
        in_specs=[pl.BlockSpec(memory_space=space) for space in ins],
        out_specs=pl.BlockSpec(memory_space=out),
        scratch_shapes=list(scratch),
        compiler_params=pltpu.CompilerParams(vmem_limit_bytes=LIMIT),
    )


VMEM, HBM = pltpu.VMEM, pltpu.HBM
TWO_SEMS = pltpu.SemaphoreType.DMA((2,))
PACK = call(pack_kernel, (1024, LANES), BF16, [HBM] * 2, VMEM, [VMEM((2, BLK, BLK), BF16), TWO_SEMS])
CORRELATE = call(
    correlate_kernel,
    (1024, LANES),
    BF16,
    [VMEM] * 4,
    VMEM,
    [VMEM((2, BLK, LANES), F32)] * 6 + [VMEM((4, LANES, LANES), F32), VMEM((BLK, LANES), F32)],
)
TOTAL = call(total_kernel, (512, LANES), BF16, [VMEM], VMEM)
UNPACK = call(unpack_kernel, (BLK, BLK), F32, [VMEM], HBM, [VMEM((BLK, BLK), F32), TWO_SEMS])


def on_device(inputs, out_grads):
    rows = PACK(*[pltpu.with_memory_space_constraint(a[0], HBM) for a in (inputs, out_grads)])
    rows = exchange(rows, HALF_GROUPS)
    parts = CORRELATE(rows, *make_tables())
    parts = exchange(parts, SUM_GROUPS)
    rows = TOTAL(parts)
    rows = exchange(rows, PLANE_GROUPS)
    return UNPACK(rows)


def solution(mesh):
    in_specs = (P("dp", "ctx", None), P("dp", "ctx", None))
    out_specs = P("ctx", None)
    return jax.shard_map(on_device, mesh=mesh, in_specs=in_specs, out_specs=out_specs, check_vma=False)
```

```python
import itertools
import math

import jax
import jax.numpy as jnp
import ml_dtypes
import numpy as np
from jax import lax
from jax.experimental import pallas as pl
from jax.experimental.pallas import tpu as pltpu
from jax.sharding import PartitionSpec as P

BLK = 256
NBLK = 32
LANES = 128
SIZES = {"x": 4, "y_lo": 2, "core": 2, "z": 8, "y_hi": 4}
F32 = jnp.float32
BF16 = jnp.bfloat16
LIMIT = 48 * 1024 * 1024


FIRST = {"x": 2, "y_lo": 0, "core": 0, "z": 5, "y_hi": 2}


def turned_range(axis):
    return [(n + FIRST[axis]) % SIZES[axis] for n in range(SIZES[axis])]


def groups_over(axes):
    rest = [a for a in SIZES if a not in axes]
    groups = []
    for fixed in itertools.product(*[range(SIZES[a]) for a in rest]):
        group = []
        for moving in itertools.product(*[turned_range(a) for a in axes]):
            place = dict(zip(rest, fixed)) | dict(zip(axes, moving))
            flat = 0
            for a in SIZES:
                flat = flat * SIZES[a] + place[a]
            group.append(flat)
        groups.append(group)
    return groups


SLOT = [0] * NBLK
for place, (z, y) in enumerate(itertools.product(turned_range("z"), turned_range("y_hi"))):
    SLOT[z * SIZES["y_hi"] + y] = place

PLANE_GROUPS = groups_over(("z", "y_hi", "y_lo", "core"))
X_GROUPS = groups_over(("x",))


def exchange(rows, groups):
    return lax.all_to_all(rows, ("dp", "ctx"), 0, 0, axis_index_groups=groups, tiled=True)


def make_tables():
    span = 2 * BLK
    freq = np.arange(BLK)[:, None]
    taps = np.arange(BLK)[None, :]
    angle = (freq * taps % span) * (2.0 * math.pi / span)
    signs = 1.0 - 2.0 * (taps % 2)
    sines = np.where(freq == 0, signs, np.sin(angle))
    forward = np.concatenate([np.cos(angle), sines], axis=0)
    weight = np.where(freq == 0, 1.0, 2.0) / span
    back = np.concatenate([weight * np.cos(angle), np.where(freq == 0, signs / span, -weight * np.sin(angle))], axis=0)
    return forward.T.astype(ml_dtypes.bfloat16), back.astype(ml_dtypes.bfloat16)


def dot(a, b):
    return jnp.dot(a, b, preferred_element_type=F32)


def permutation(source_of):
    row = lax.broadcasted_iota(jnp.int32, (BLK, BLK), 0)
    col = lax.broadcasted_iota(jnp.int32, (BLK, BLK), 1)
    return jnp.where(col == source_of(row), 1.0, 0.0).astype(BF16)


def pack_kernel(in_hbm, grad_hbm, out_ref, held, sems):
    copies = [pltpu.make_async_copy(ref, held.at[a], sems.at[a]) for a, ref in enumerate((in_hbm, grad_hbm))]
    for copy in copies:
        copy.start()
    perm = permutation(lambda m: (m & 7) * 32 + (m >> 3))
    turned = []
    for a in range(2):
        copies[a].wait()
        turned.append(jnp.transpose(held[a]))
    for part in range(4):
        pieces = []
        for a in range(2):
            for c in range(2):
                for th in range(2):
                    start = c * LANES + part * 32
                    pieces.append(turned[a][start : start + 32, th * LANES : (th + 1) * LANES])
        out_ref[part * BLK : (part + 1) * BLK, :] = dot(perm, jnp.concatenate(pieces, axis=0)).astype(BF16)


def correlate_kernel(rows_ref, forward_ref, back_ref, out_ref, xa, xb, xc, ga, gb, gc, zed, ybuf):
    def source(m):
        a, th, j8, r, c = m >> 7, (m >> 6) & 1, (m >> 3) & 7, (m >> 1) & 3, m & 1
        return j8 * 32 + r * 8 + a * 4 + c * 2 + th

    perm = permutation(source)
    blocks = [[], []]
    for part in range(4):
        q = dot(perm, rows_ref[part * BLK : (part + 1) * BLK, :]).astype(BF16)
        for a in range(2):
            at = a * 128
            blocks[a].append(jnp.concatenate([q[at : at + 64], q[at + 64 : at + 128]], axis=1))
    first = lax.broadcasted_iota(jnp.int32, (BLK, LANES), 1) == 0
    forward = forward_ref[...]
    spec_in = dot(jnp.concatenate(blocks[0], axis=0), forward).astype(BF16).astype(F32)
    spec_grad = dot(jnp.concatenate(blocks[1], axis=0), forward).astype(BF16).astype(F32)
    for half in range(2):
        up = slice(half * LANES, (half + 1) * LANES)
        down = slice(BLK + half * LANES, BLK + (half + 1) * LANES)
        cos_in, sin_in = spec_in[:, up], spec_in[:, down]
        cos_grad, sin_grad = spec_grad[:, up], spec_grad[:, down]
        x_a, x_b, x_c = cos_in + sin_in, sin_in, cos_in
        g_a, g_b, g_c = cos_grad, cos_grad - sin_grad, cos_grad + sin_grad
        if half == 0:
            x_a = jnp.where(first, 0.0, x_a)
            x_b = jnp.where(first, -cos_in, x_b)
            x_c = jnp.where(first, -sin_in, x_c)
            g_b = jnp.where(first, cos_grad, g_b)
            g_c = jnp.where(first, sin_grad, g_c)
        for ref, value in ((xa, x_a), (xb, x_b), (xc, x_c), (ga, g_a), (gb, g_b), (gc, g_c)):
            ref[half] = value

    sign = jnp.where(lax.broadcasted_iota(jnp.int32, (8, LANES), 1) % 2 == 0, 1.0, -1.0)
    width = 4

    for half in range(2):
        def at(ref, j):
            return ref[half, SLOT[j] * 8 : (SLOT[j] + 1) * 8, :]

        after = [jnp.zeros((8, LANES), F32)] * 2
        for k0 in reversed(range(0, NBLK, width)):
            sums = [[None] * width for _ in range(3)]
            for i in range(k0, NBLK):
                grads = [at(ref, i) for ref in (ga, gb, gc)]
                for kk in range(width):
                    j = i - k0 - kk
                    if j < 0:
                        continue
                    for n, ref in enumerate((xa, xb, xc)):
                        product = grads[n] * at(ref, j)
                        sums[n][kk] = product if sums[n][kk] is None else sums[n][kk] + product
            for kk in reversed(range(width)):
                k = k0 + kk
                now = [sums[0][kk] - sums[1][kk], sums[0][kk] - sums[2][kk]]
                for part in range(2):
                    total = now[part] + sign * after[part]
                    total = total + pltpu.roll(total, 4, 0)
                    total = total + pltpu.roll(total, 2, 0)
                    zed[part * 2 + half, 2 * SLOT[k] : 2 * SLOT[k] + 2, :] = total[0:2]
                after = now
    z = jnp.concatenate([zed[n] for n in range(4)], axis=1)
    y = dot(z.astype(BF16), back_ref[...])
    for lh in range(2):
        ybuf[pl.ds(lh, 64, stride=2), :] = y[:, lh * LANES : (lh + 1) * LANES]
    y = ybuf[...].astype(BF16)
    for x in range(4):
        out_ref[x * LANES : (x + 1) * LANES, :] = y


def total_kernel(parts_ref, out_ref):
    total = parts_ref[0:LANES].astype(F32)
    for n in range(1, 4):
        total = total + parts_ref[n * LANES : (n + 1) * LANES].astype(F32)
    row = lax.broadcasted_iota(jnp.int32, (512, LANES), 0)
    col = lax.broadcasted_iota(jnp.int32, (512, LANES), 1)
    repeat = jnp.where(col == (row >> 4) * 4 + (row & 3), 1.0, 0.0).astype(BF16)
    out_ref[...] = dot(repeat, total.astype(BF16)).astype(BF16)


def unpack_kernel(rows_ref, out_hbm, held, sems):
    perm = permutation(lambda m: (m & 63) * 4 + (m >> 6))
    halves = [dot(perm, rows_ref[part * BLK : (part + 1) * BLK, :]) for part in range(2)]
    copies = []
    for lh in range(2):
        rows = slice(lh * LANES, (lh + 1) * LANES)
        for c in range(2):
            at = (c * 2 + lh) * 64
            block = jnp.concatenate([halves[part][at : at + 64] for part in range(2)], axis=0)
            held[rows, c * LANES : (c + 1) * LANES] = jnp.transpose(block)
        copies.append(pltpu.make_async_copy(held.at[rows], out_hbm.at[rows], sems.at[lh]))
        copies[-1].start()
    for copy in copies:
        copy.wait()


def call(kernel, shape, dtype, ins, out, scratch=()):
    return pl.pallas_call(
        kernel,
        out_shape=jax.ShapeDtypeStruct(shape, dtype),
        in_specs=[pl.BlockSpec(memory_space=space) for space in ins],
        out_specs=pl.BlockSpec(memory_space=out),
        scratch_shapes=list(scratch),
        compiler_params=pltpu.CompilerParams(vmem_limit_bytes=LIMIT),
    )


VMEM, HBM = pltpu.VMEM, pltpu.HBM
TWO_SEMS = pltpu.SemaphoreType.DMA((2,))
PACK = call(pack_kernel, (1024, LANES), BF16, [HBM] * 2, VMEM, [VMEM((2, BLK, BLK), BF16), TWO_SEMS])
CORRELATE = call(
    correlate_kernel,
    (512, LANES),
    BF16,
    [VMEM] * 3,
    VMEM,
    [VMEM((2, BLK, LANES), F32)] * 6 + [VMEM((4, 64, LANES), F32), VMEM((LANES, LANES), F32)],
)
TOTAL = call(total_kernel, (512, LANES), BF16, [VMEM], VMEM)
UNPACK = call(unpack_kernel, (BLK, BLK), F32, [VMEM], HBM, [VMEM((BLK, BLK), F32), TWO_SEMS])


def on_device(inputs, out_grads):
    rows = PACK(*[pltpu.with_memory_space_constraint(a[0], HBM) for a in (inputs, out_grads)])
    rows = exchange(rows, PLANE_GROUPS)
    parts = CORRELATE(rows, *make_tables())
    parts = exchange(parts, X_GROUPS)
    rows = TOTAL(parts)
    rows = exchange(rows, PLANE_GROUPS)
    return UNPACK(rows)


def solution(mesh):
    in_specs = (P("dp", "ctx", None), P("dp", "ctx", None))
    out_specs = P("ctx", None)
    return jax.shard_map(on_device, mesh=mesh, in_specs=in_specs, out_specs=out_specs, check_vma=False)
```

```python
import itertools
import math

import jax
import jax.numpy as jnp
import ml_dtypes
import numpy as np
from jax import lax
from jax.experimental import pallas as pl
from jax.experimental.pallas import tpu as pltpu
from jax.sharding import PartitionSpec as P

BLK = 256
NBLK = 32
LANES = 128
SIZES = {"x": 4, "y_lo": 2, "core": 2, "z": 8, "y_hi": 4}
F32 = jnp.float32
BF16 = jnp.bfloat16
LIMIT = 48 * 1024 * 1024


FIRST = {"x": 2, "y_lo": 0, "core": 1, "z": 5, "y_hi": 2}


def turned_range(axis):
    return [(n + FIRST[axis]) % SIZES[axis] for n in range(SIZES[axis])]


def groups_over(axes):
    rest = [a for a in SIZES if a not in axes]
    groups = []
    for fixed in itertools.product(*[range(SIZES[a]) for a in rest]):
        group = []
        for moving in itertools.product(*[turned_range(a) for a in axes]):
            place = dict(zip(rest, fixed)) | dict(zip(axes, moving))
            flat = 0
            for a in SIZES:
                flat = flat * SIZES[a] + place[a]
            group.append(flat)
        groups.append(group)
    return groups


SLOT = [0] * NBLK
for place, (z, y) in enumerate(itertools.product(turned_range("z"), turned_range("y_hi"))):
    SLOT[z * SIZES["y_hi"] + y] = place

PLANE_GROUPS = groups_over(("z", "y_hi", "y_lo", "core"))
X_GROUPS = groups_over(("x",))


def exchange(rows, groups):
    return lax.all_to_all(rows, ("dp", "ctx"), 0, 0, axis_index_groups=groups, tiled=True)


def make_tables():
    span = 2 * BLK
    freq = np.arange(BLK)[:, None]
    taps = np.arange(BLK)[None, :]
    angle = (freq * taps % span) * (2.0 * math.pi / span)
    signs = 1.0 - 2.0 * (taps % 2)
    sines = np.where(freq == 0, signs, np.sin(angle))
    forward = np.concatenate([np.cos(angle), sines], axis=0)
    weight = np.where(freq == 0, 1.0, 2.0) / span
    back = np.concatenate([weight * np.cos(angle), np.where(freq == 0, signs / span, -weight * np.sin(angle))], axis=0)
    return forward.T.astype(ml_dtypes.bfloat16), back.astype(ml_dtypes.bfloat16)


def dot(a, b):
    return jnp.dot(a, b, preferred_element_type=F32)


def permutation(source_of):
    row = lax.broadcasted_iota(jnp.int32, (BLK, BLK), 0)
    col = lax.broadcasted_iota(jnp.int32, (BLK, BLK), 1)
    return jnp.where(col == source_of(row), 1.0, 0.0).astype(BF16)


def pack_kernel(in_hbm, grad_hbm, out_ref, held, sems):
    copies = [pltpu.make_async_copy(ref, held.at[a], sems.at[a]) for a, ref in enumerate((in_hbm, grad_hbm))]
    for copy in copies:
        copy.start()
    perm = permutation(lambda m: (m & 7) * 32 + (m >> 3))
    turned = []
    for a in range(2):
        copies[a].wait()
        turned.append(jnp.transpose(held[a]))
    for part in range(4):
        pieces = []
        for a in range(2):
            for c in range(2):
                for th in range(2):
                    start = c * LANES + part * 32
                    pieces.append(turned[a][start : start + 32, th * LANES : (th + 1) * LANES])
        out_ref[part * BLK : (part + 1) * BLK, :] = dot(perm, jnp.concatenate(pieces, axis=0)).astype(BF16)


def correlate_kernel(rows_ref, forward_ref, back_ref, out_ref, xa, xb, xc, ga, gb, gc, zed, ybuf):
    def source(m):
        a, th, j8, r, c = m >> 7, (m >> 6) & 1, (m >> 3) & 7, (m >> 1) & 3, m & 1
        return j8 * 32 + r * 8 + a * 4 + c * 2 + th

    perm = permutation(source)
    blocks = [[], []]
    for part in range(4):
        q = dot(perm, rows_ref[part * BLK : (part + 1) * BLK, :]).astype(BF16)
        for a in range(2):
            at = a * 128
            blocks[a].append(jnp.concatenate([q[at : at + 64], q[at + 64 : at + 128]], axis=1))
    first = lax.broadcasted_iota(jnp.int32, (BLK, LANES), 1) == 0
    forward = forward_ref[...]
    spec_in = dot(jnp.concatenate(blocks[0], axis=0), forward).astype(BF16).astype(F32)
    spec_grad = dot(jnp.concatenate(blocks[1], axis=0), forward).astype(BF16).astype(F32)
    for half in range(2):
        up = slice(half * LANES, (half + 1) * LANES)
        down = slice(BLK + half * LANES, BLK + (half + 1) * LANES)
        cos_in, sin_in = spec_in[:, up], spec_in[:, down]
        cos_grad, sin_grad = spec_grad[:, up], spec_grad[:, down]
        x_a, x_b, x_c = cos_in + sin_in, sin_in, cos_in
        g_a, g_b, g_c = cos_grad, cos_grad - sin_grad, cos_grad + sin_grad
        if half == 0:
            x_a = jnp.where(first, 0.0, x_a)
            x_b = jnp.where(first, -cos_in, x_b)
            x_c = jnp.where(first, -sin_in, x_c)
            g_b = jnp.where(first, cos_grad, g_b)
            g_c = jnp.where(first, sin_grad, g_c)
        for ref, value in ((xa, x_a), (xb, x_b), (xc, x_c), (ga, g_a), (gb, g_b), (gc, g_c)):
            ref[half] = value

    sign = jnp.where(lax.broadcasted_iota(jnp.int32, (8, LANES), 1) % 2 == 0, 1.0, -1.0)
    width = 4

    for half in range(2):
        def at(ref, j):
            return ref[half, SLOT[j] * 8 : (SLOT[j] + 1) * 8, :]

        after = [jnp.zeros((8, LANES), F32)] * 2
        for k0 in reversed(range(0, NBLK, width)):
            sums = [[None] * width for _ in range(3)]
            for i in range(k0, NBLK):
                grads = [at(ref, i) for ref in (ga, gb, gc)]
                for kk in range(width):
                    j = i - k0 - kk
                    if j < 0:
                        continue
                    for n, ref in enumerate((xa, xb, xc)):
                        product = grads[n] * at(ref, j)
                        sums[n][kk] = product if sums[n][kk] is None else sums[n][kk] + product
            for kk in reversed(range(width)):
                k = k0 + kk
                now = [sums[0][kk] - sums[1][kk], sums[0][kk] - sums[2][kk]]
                for part in range(2):
                    total = now[part] + sign * after[part]
                    total = total + pltpu.roll(total, 4, 0)
                    total = total + pltpu.roll(total, 2, 0)
                    zed[part * 2 + half, 2 * SLOT[k] : 2 * SLOT[k] + 2, :] = total[0:2]
                after = now
    z = jnp.concatenate([zed[n] for n in range(4)], axis=1)
    y = dot(z.astype(BF16), back_ref[...])
    for lh in range(2):
        ybuf[pl.ds(lh, 64, stride=2), :] = y[:, lh * LANES : (lh + 1) * LANES]
    y = ybuf[...].astype(BF16)
    for x in range(4):
        out_ref[x * LANES : (x + 1) * LANES, :] = y


def total_kernel(parts_ref, out_ref):
    total = parts_ref[0:LANES].astype(F32)
    for n in range(1, 4):
        total = total + parts_ref[n * LANES : (n + 1) * LANES].astype(F32)
    row = lax.broadcasted_iota(jnp.int32, (512, LANES), 0)
    col = lax.broadcasted_iota(jnp.int32, (512, LANES), 1)
    repeat = jnp.where(col == (row >> 4) * 4 + (row & 3), 1.0, 0.0).astype(BF16)
    out_ref[...] = dot(repeat, total.astype(BF16)).astype(BF16)


def unpack_kernel(rows_ref, out_hbm, held, sems):
    perm = permutation(lambda m: (m & 63) * 4 + (m >> 6))
    halves = [dot(perm, rows_ref[part * BLK : (part + 1) * BLK, :]) for part in range(2)]
    copies = []
    for lh in range(2):
        rows = slice(lh * LANES, (lh + 1) * LANES)
        for c in range(2):
            at = (c * 2 + lh) * 64
            block = jnp.concatenate([halves[part][at : at + 64] for part in range(2)], axis=0)
            held[rows, c * LANES : (c + 1) * LANES] = jnp.transpose(block)
        copies.append(pltpu.make_async_copy(held.at[rows], out_hbm.at[rows], sems.at[lh]))
        copies[-1].start()
    for copy in copies:
        copy.wait()


def call(kernel, shape, dtype, ins, out, scratch=()):
    return pl.pallas_call(
        kernel,
        out_shape=jax.ShapeDtypeStruct(shape, dtype),
        in_specs=[pl.BlockSpec(memory_space=space) for space in ins],
        out_specs=pl.BlockSpec(memory_space=out),
        scratch_shapes=list(scratch),
        compiler_params=pltpu.CompilerParams(vmem_limit_bytes=LIMIT),
    )


VMEM, HBM = pltpu.VMEM, pltpu.HBM
TWO_SEMS = pltpu.SemaphoreType.DMA((2,))
PACK = call(pack_kernel, (1024, LANES), BF16, [HBM] * 2, VMEM, [VMEM((2, BLK, BLK), BF16), TWO_SEMS])
CORRELATE = call(
    correlate_kernel,
    (512, LANES),
    BF16,
    [VMEM] * 3,
    VMEM,
    [VMEM((2, BLK, LANES), F32)] * 6 + [VMEM((4, 64, LANES), F32), VMEM((LANES, LANES), F32)],
)
TOTAL = call(total_kernel, (512, LANES), BF16, [VMEM], VMEM)
UNPACK = call(unpack_kernel, (BLK, BLK), F32, [VMEM], HBM, [VMEM((BLK, BLK), F32), TWO_SEMS])


def on_device(inputs, out_grads):
    rows = PACK(*[pltpu.with_memory_space_constraint(a[0], HBM) for a in (inputs, out_grads)])
    rows = exchange(rows, PLANE_GROUPS)
    parts = CORRELATE(rows, *make_tables())
    parts = exchange(parts, X_GROUPS)
    rows = TOTAL(parts)
    rows = exchange(rows, PLANE_GROUPS)
    return UNPACK(rows)


def solution(mesh):
    in_specs = (P("dp", "ctx", None), P("dp", "ctx", None))
    out_specs = P("ctx", None)
    return jax.shard_map(on_device, mesh=mesh, in_specs=in_specs, out_specs=out_specs, check_vma=False)
```

```python
import itertools
import math

import jax
import jax.numpy as jnp
import ml_dtypes
import numpy as np
from jax import lax
from jax.experimental import pallas as pl
from jax.experimental.pallas import tpu as pltpu
from jax.sharding import PartitionSpec as P

BLK = 256
NBLK = 32
LANES = 128
SIZES = {"x": 4, "y_lo": 2, "core": 2, "z": 8, "y_hi": 4}
F32 = jnp.float32
BF16 = jnp.bfloat16
LIMIT = 48 * 1024 * 1024


FIRST = {"x": 2, "y_lo": 0, "core": 1, "z": 5, "y_hi": 2}


def turned_range(axis):
    return [(n + FIRST[axis]) % SIZES[axis] for n in range(SIZES[axis])]


def groups_over(axes):
    rest = [a for a in SIZES if a not in axes]
    groups = []
    for fixed in itertools.product(*[range(SIZES[a]) for a in rest]):
        group = []
        for moving in itertools.product(*[turned_range(a) for a in axes]):
            place = dict(zip(rest, fixed)) | dict(zip(axes, moving))
            flat = 0
            for a in SIZES:
                flat = flat * SIZES[a] + place[a]
            group.append(flat)
        groups.append(group)
    return groups


SLOT = [0] * NBLK
for place, (z, y) in enumerate(itertools.product(turned_range("z"), turned_range("y_hi"))):
    SLOT[z * SIZES["y_hi"] + y] = place

PLANE_GROUPS = groups_over(("core", "z", "y_hi", "y_lo"))
X_GROUPS = groups_over(("x",))


def exchange(rows, groups):
    return lax.all_to_all(rows, ("dp", "ctx"), 0, 0, axis_index_groups=groups, tiled=True)


def make_tables():
    span = 2 * BLK
    freq = np.arange(BLK)[:, None]
    taps = np.arange(BLK)[None, :]
    angle = (freq * taps % span) * (2.0 * math.pi / span)
    signs = 1.0 - 2.0 * (taps % 2)
    sines = np.where(freq == 0, signs, np.sin(angle))
    forward = np.concatenate([np.cos(angle), sines], axis=0)
    weight = np.where(freq == 0, 1.0, 2.0) / span
    back = np.concatenate([weight * np.cos(angle), np.where(freq == 0, signs / span, -weight * np.sin(angle))], axis=0)
    return forward.T.astype(ml_dtypes.bfloat16), back.astype(ml_dtypes.bfloat16)


def dot(a, b):
    return jnp.dot(a, b, preferred_element_type=F32)


def permutation(source_of):
    row = lax.broadcasted_iota(jnp.int32, (BLK, BLK), 0)
    col = lax.broadcasted_iota(jnp.int32, (BLK, BLK), 1)
    return jnp.where(col == source_of(row), 1.0, 0.0).astype(BF16)


def pack_kernel(in_hbm, grad_hbm, out_ref, held, sems):
    copies = [pltpu.make_async_copy(ref, held.at[a], sems.at[a]) for a, ref in enumerate((in_hbm, grad_hbm))]
    for copy in copies:
        copy.start()
    perm = permutation(lambda m: (m & 7) * 32 + (m >> 3))
    turned = []
    for a in range(2):
        copies[a].wait()
        turned.append(jnp.transpose(held[a]))
    for part in range(4):
        pieces = []
        for a in range(2):
            for c in range(2):
                for th in range(2):
                    start = c * LANES + part * 32
                    pieces.append(turned[a][start : start + 32, th * LANES : (th + 1) * LANES])
        out_ref[part * BLK : (part + 1) * BLK, :] = dot(perm, jnp.concatenate(pieces, axis=0)).astype(BF16)


def correlate_kernel(rows_ref, forward_ref, back_ref, out_ref, xa, xb, xc, ga, gb, gc, zed, ybuf):
    def source(m):
        a, th, j8, core, y, c = m >> 7, (m >> 6) & 1, (m >> 3) & 7, (m >> 2) & 1, (m >> 1) & 1, m & 1
        return core * 128 + (j8 * 2 + y) * 8 + a * 4 + c * 2 + th

    perm = permutation(source)
    blocks = [[], []]
    for part in range(4):
        both = [rows_ref[core * 512 + part * LANES : core * 512 + (part + 1) * LANES, :] for core in range(2)]
        q = dot(perm, jnp.concatenate(both, axis=0)).astype(BF16)
        for a in range(2):
            at = a * 128
            blocks[a].append(jnp.concatenate([q[at : at + 64], q[at + 64 : at + 128]], axis=1))
    first = lax.broadcasted_iota(jnp.int32, (BLK, LANES), 1) == 0
    forward = forward_ref[...]
    spec_in = dot(jnp.concatenate(blocks[0], axis=0), forward).astype(BF16).astype(F32)
    spec_grad = dot(jnp.concatenate(blocks[1], axis=0), forward).astype(BF16).astype(F32)
    for half in range(2):
        up = slice(half * LANES, (half + 1) * LANES)
        down = slice(BLK + half * LANES, BLK + (half + 1) * LANES)
        cos_in, sin_in = spec_in[:, up], spec_in[:, down]
        cos_grad, sin_grad = spec_grad[:, up], spec_grad[:, down]
        x_a, x_b, x_c = cos_in + sin_in, sin_in, cos_in
        g_a, g_b, g_c = cos_grad, cos_grad - sin_grad, cos_grad + sin_grad
        if half == 0:
            x_a = jnp.where(first, 0.0, x_a)
            x_b = jnp.where(first, -cos_in, x_b)
            x_c = jnp.where(first, -sin_in, x_c)
            g_b = jnp.where(first, cos_grad, g_b)
            g_c = jnp.where(first, sin_grad, g_c)
        for ref, value in ((xa, x_a), (xb, x_b), (xc, x_c), (ga, g_a), (gb, g_b), (gc, g_c)):
            ref[half] = value

    sign = jnp.where(lax.broadcasted_iota(jnp.int32, (8, LANES), 1) % 2 == 0, 1.0, -1.0)
    width = 4

    for half in range(2):
        def at(ref, j):
            return ref[half, SLOT[j] * 8 : (SLOT[j] + 1) * 8, :]

        after = [jnp.zeros((8, LANES), F32)] * 2
        for k0 in reversed(range(0, NBLK, width)):
            sums = [[None] * width for _ in range(3)]
            for i in range(k0, NBLK):
                grads = [at(ref, i) for ref in (ga, gb, gc)]
                for kk in range(width):
                    j = i - k0 - kk
                    if j < 0:
                        continue
                    for n, ref in enumerate((xa, xb, xc)):
                        product = grads[n] * at(ref, j)
                        sums[n][kk] = product if sums[n][kk] is None else sums[n][kk] + product
            for kk in reversed(range(width)):
                k = k0 + kk
                now = [sums[0][kk] - sums[1][kk], sums[0][kk] - sums[2][kk]]
                for part in range(2):
                    total = now[part] + sign * after[part]
                    total = total + pltpu.roll(total, 4, 0)
                    total = total + pltpu.roll(total, 2, 0)
                    zed[part * 2 + half, 2 * SLOT[k] : 2 * SLOT[k] + 2, :] = total[0:2]
                after = now
    z = jnp.concatenate([zed[n] for n in range(4)], axis=1)
    y = dot(z.astype(BF16), back_ref[...])
    for lh in range(2):
        ybuf[pl.ds(lh, 64, stride=2), :] = y[:, lh * LANES : (lh + 1) * LANES]
    y = ybuf[...].astype(BF16)
    for x in range(4):
        out_ref[x * LANES : (x + 1) * LANES, :] = y


def total_kernel(parts_ref, out_ref):
    total = parts_ref[0:LANES].astype(F32)
    for n in range(1, 4):
        total = total + parts_ref[n * LANES : (n + 1) * LANES].astype(F32)
    row = lax.broadcasted_iota(jnp.int32, (512, LANES), 0)
    col = lax.broadcasted_iota(jnp.int32, (512, LANES), 1)
    repeat = jnp.where(col == ((row >> 3) & 31) * 4 + (row & 3), 1.0, 0.0).astype(BF16)
    out_ref[...] = dot(repeat, total.astype(BF16)).astype(BF16)


def unpack_kernel(rows_ref, out_hbm, held, sems):
    perm = permutation(lambda m: (m & 63) * 4 + (m >> 6))
    halves = [dot(perm, rows_ref[part * BLK : (part + 1) * BLK, :]) for part in range(2)]
    copies = []
    for lh in range(2):
        rows = slice(lh * LANES, (lh + 1) * LANES)
        for c in range(2):
            at = (c * 2 + lh) * 64
            block = jnp.concatenate([halves[part][at : at + 64] for part in range(2)], axis=0)
            held[rows, c * LANES : (c + 1) * LANES] = jnp.transpose(block)
        copies.append(pltpu.make_async_copy(held.at[rows], out_hbm.at[rows], sems.at[lh]))
        copies[-1].start()
    for copy in copies:
        copy.wait()


def call(kernel, shape, dtype, ins, out, scratch=()):
    return pl.pallas_call(
        kernel,
        out_shape=jax.ShapeDtypeStruct(shape, dtype),
        in_specs=[pl.BlockSpec(memory_space=space) for space in ins],
        out_specs=pl.BlockSpec(memory_space=out),
        scratch_shapes=list(scratch),
        compiler_params=pltpu.CompilerParams(vmem_limit_bytes=LIMIT),
    )


VMEM, HBM = pltpu.VMEM, pltpu.HBM
TWO_SEMS = pltpu.SemaphoreType.DMA((2,))
PACK = call(pack_kernel, (1024, LANES), BF16, [HBM] * 2, VMEM, [VMEM((2, BLK, BLK), BF16), TWO_SEMS])
CORRELATE = call(
    correlate_kernel,
    (512, LANES),
    BF16,
    [VMEM] * 3,
    VMEM,
    [VMEM((2, BLK, LANES), F32)] * 6 + [VMEM((4, 64, LANES), F32), VMEM((LANES, LANES), F32)],
)
TOTAL = call(total_kernel, (512, LANES), BF16, [VMEM], VMEM)
UNPACK = call(unpack_kernel, (BLK, BLK), F32, [VMEM], HBM, [VMEM((BLK, BLK), F32), TWO_SEMS])


def on_device(inputs, out_grads):
    rows = PACK(*[pltpu.with_memory_space_constraint(a[0], HBM) for a in (inputs, out_grads)])
    rows = exchange(rows, PLANE_GROUPS)
    parts = CORRELATE(rows, *make_tables())
    parts = exchange(parts, X_GROUPS)
    rows = TOTAL(parts)
    rows = exchange(rows, PLANE_GROUPS)
    return UNPACK(rows)


def solution(mesh):
    in_specs = (P("dp", "ctx", None), P("dp", "ctx", None))
    out_specs = P("ctx", None)
    return jax.shard_map(on_device, mesh=mesh, in_specs=in_specs, out_specs=out_specs, check_vma=False)
```

```python
import itertools
import math

import jax
import jax.numpy as jnp
import ml_dtypes
import numpy as np
from jax import lax
from jax.experimental import pallas as pl
from jax.experimental.pallas import tpu as pltpu
from jax.sharding import PartitionSpec as P

BLK = 256
NBLK = 32
LANES = 128
SIZES = {"x": 4, "y_lo": 2, "core": 2, "z": 8, "y_hi": 4}
F32 = jnp.float32
BF16 = jnp.bfloat16
LIMIT = 48 * 1024 * 1024


ORDER = {
    "x": (2, 0, 1, 3),
    "y_lo": (0, 1),
    "core": (1, 0),
    "z": (5, 6, 7, 0, 1, 2, 3, 4),
    "y_hi": (2, 3, 0, 1),
}


def groups_over(axes):
    rest = [a for a in SIZES if a not in axes]
    groups = []
    for fixed in itertools.product(*[range(SIZES[a]) for a in rest]):
        group = []
        for moving in itertools.product(*[ORDER[a] for a in axes]):
            place = dict(zip(rest, fixed)) | dict(zip(axes, moving))
            flat = 0
            for a in SIZES:
                flat = flat * SIZES[a] + place[a]
            group.append(flat)
        groups.append(group)
    return groups


SLOT = [0] * NBLK
for place, (z, y) in enumerate(itertools.product(ORDER["z"], ORDER["y_hi"])):
    SLOT[z * SIZES["y_hi"] + y] = place

PLANE_GROUPS = groups_over(("core", "z", "y_hi", "y_lo"))
X_GROUPS = groups_over(("x",))


def exchange(rows, groups):
    return lax.all_to_all(rows, ("dp", "ctx"), 0, 0, axis_index_groups=groups, tiled=True)


def make_tables():
    span = 2 * BLK
    freq = np.arange(BLK)[:, None]
    taps = np.arange(BLK)[None, :]
    angle = (freq * taps % span) * (2.0 * math.pi / span)
    signs = 1.0 - 2.0 * (taps % 2)
    sines = np.where(freq == 0, signs, np.sin(angle))
    forward = np.concatenate([np.cos(angle), sines], axis=0)
    weight = np.where(freq == 0, 1.0, 2.0) / span
    back = np.concatenate([weight * np.cos(angle), np.where(freq == 0, signs / span, -weight * np.sin(angle))], axis=0)
    return forward.T.astype(ml_dtypes.bfloat16), back.astype(ml_dtypes.bfloat16)


def dot(a, b):
    return jnp.dot(a, b, preferred_element_type=F32)


def permutation(source_of):
    row = lax.broadcasted_iota(jnp.int32, (BLK, BLK), 0)
    col = lax.broadcasted_iota(jnp.int32, (BLK, BLK), 1)
    return jnp.where(col == source_of(row), 1.0, 0.0).astype(BF16)


def one_hot(rows, cols, source_of):
    return (np.arange(cols)[None, :] == source_of(np.arange(rows))[:, None]).astype(ml_dtypes.bfloat16)


def pack_kernel(in_hbm, grad_hbm, out_ref, held, sems):
    copies = [pltpu.make_async_copy(ref, held.at[a], sems.at[a]) for a, ref in enumerate((in_hbm, grad_hbm))]
    for copy in copies:
        copy.start()
    perm = permutation(lambda m: (m & 7) * 32 + (m >> 3))
    turned = []
    for a in range(2):
        copies[a].wait()
        turned.append(jnp.transpose(held[a]))
    for part in range(4):
        pieces = []
        for a in range(2):
            for c in range(2):
                for th in range(2):
                    start = c * LANES + part * 32
                    pieces.append(turned[a][start : start + 32, th * LANES : (th + 1) * LANES])
        out_ref[part * BLK : (part + 1) * BLK, :] = dot(perm, jnp.concatenate(pieces, axis=0)).astype(BF16)


def correlate_source(m):
    a, th, j8, core, y, c = m >> 7, (m >> 6) & 1, (m >> 3) & 7, (m >> 2) & 1, (m >> 1) & 1, m & 1
    return core * 128 + (j8 * 2 + y) * 8 + a * 4 + c * 2 + th


def correlate_kernel(rows_ref, perm_ref, forward_ref, back_ref, out_ref, xa, xb, xc, ga, gb, gc, zed, ybuf):
    perm = perm_ref[...]
    blocks = [[], []]
    for part in range(4):
        both = [rows_ref[core * 512 + part * LANES : core * 512 + (part + 1) * LANES, :] for core in range(2)]
        q = dot(perm, jnp.concatenate(both, axis=0)).astype(BF16)
        for a in range(2):
            at = a * 128
            blocks[a].append(jnp.concatenate([q[at : at + 64], q[at + 64 : at + 128]], axis=1))
    first = lax.broadcasted_iota(jnp.int32, (BLK, LANES), 1) == 0
    forward = forward_ref[...]
    spec_in = dot(jnp.concatenate(blocks[0], axis=0), forward).astype(BF16).astype(F32)
    spec_grad = dot(jnp.concatenate(blocks[1], axis=0), forward).astype(BF16).astype(F32)
    for half in range(2):
        up = slice(half * LANES, (half + 1) * LANES)
        down = slice(BLK + half * LANES, BLK + (half + 1) * LANES)
        cos_in, sin_in = spec_in[:, up], spec_in[:, down]
        cos_grad, sin_grad = spec_grad[:, up], spec_grad[:, down]
        x_a, x_b, x_c = cos_in + sin_in, sin_in, cos_in
        g_a, g_b, g_c = cos_grad, cos_grad - sin_grad, cos_grad + sin_grad
        if half == 0:
            x_a = jnp.where(first, 0.0, x_a)
            x_b = jnp.where(first, -cos_in, x_b)
            x_c = jnp.where(first, -sin_in, x_c)
            g_b = jnp.where(first, cos_grad, g_b)
            g_c = jnp.where(first, sin_grad, g_c)
        for ref, value in ((xa, x_a), (xb, x_b), (xc, x_c), (ga, g_a), (gb, g_b), (gc, g_c)):
            ref[half] = value

    sign = jnp.where(lax.broadcasted_iota(jnp.int32, (8, LANES), 1) % 2 == 0, 1.0, -1.0)
    width = 4

    for half in range(2):
        def at(ref, j):
            return ref[half, SLOT[j] * 8 : (SLOT[j] + 1) * 8, :]

        after = [jnp.zeros((8, LANES), F32)] * 2
        for k0 in reversed(range(0, NBLK, width)):
            sums = [[None] * width for _ in range(3)]
            for i in range(k0, NBLK):
                grads = [at(ref, i) for ref in (ga, gb, gc)]
                for kk in range(width):
                    j = i - k0 - kk
                    if j < 0:
                        continue
                    for n, ref in enumerate((xa, xb, xc)):
                        product = grads[n] * at(ref, j)
                        sums[n][kk] = product if sums[n][kk] is None else sums[n][kk] + product
            for kk in reversed(range(width)):
                k = k0 + kk
                now = [sums[0][kk] - sums[1][kk], sums[0][kk] - sums[2][kk]]
                for part in range(2):
                    total = now[part] + sign * after[part]
                    total = total + pltpu.roll(total, 4, 0)
                    total = total + pltpu.roll(total, 2, 0)
                    zed[part * 2 + half, 2 * SLOT[k] : 2 * SLOT[k] + 2, :] = total[0:2]
                after = now
    z = jnp.concatenate([zed[n] for n in range(4)], axis=1)
    y = dot(z.astype(BF16), back_ref[...])
    for lh in range(2):
        ybuf[pl.ds(lh, 64, stride=2), :] = y[:, lh * LANES : (lh + 1) * LANES]
    y = ybuf[...].astype(BF16)
    for x in range(4):
        out_ref[x * LANES : (x + 1) * LANES, :] = y


def total_source(m):
    return ((m >> 3) & 31) * 4 + (m & 3)


def total_kernel(parts_ref, repeat_ref, out_ref):
    total = parts_ref[0:LANES].astype(F32)
    for n in range(1, 4):
        total = total + parts_ref[n * LANES : (n + 1) * LANES].astype(F32)
    out_ref[...] = dot(repeat_ref[...], total.astype(BF16)).astype(BF16)


def unpack_source(m):
    return (m & 63) * 4 + (m >> 6)


def unpack_kernel(rows_ref, perm_ref, out_hbm, held, sems):
    perm = perm_ref[...]
    halves = [dot(perm, rows_ref[part * BLK : (part + 1) * BLK, :]) for part in range(2)]
    copies = []
    for lh in range(2):
        rows = slice(lh * LANES, (lh + 1) * LANES)
        for c in range(2):
            at = (c * 2 + lh) * 64
            block = jnp.concatenate([halves[part][at : at + 64] for part in range(2)], axis=0)
            held[rows, c * LANES : (c + 1) * LANES] = jnp.transpose(block)
        copies.append(pltpu.make_async_copy(held.at[rows], out_hbm.at[rows], sems.at[lh]))
        copies[-1].start()
    for copy in copies:
        copy.wait()


def call(kernel, shape, dtype, ins, out, scratch=()):
    return pl.pallas_call(
        kernel,
        out_shape=jax.ShapeDtypeStruct(shape, dtype),
        in_specs=[pl.BlockSpec(memory_space=space) for space in ins],
        out_specs=pl.BlockSpec(memory_space=out),
        scratch_shapes=list(scratch),
        compiler_params=pltpu.CompilerParams(vmem_limit_bytes=LIMIT),
    )


VMEM, HBM = pltpu.VMEM, pltpu.HBM
TWO_SEMS = pltpu.SemaphoreType.DMA((2,))
PACK = call(pack_kernel, (1024, LANES), BF16, [HBM] * 2, VMEM, [VMEM((2, BLK, BLK), BF16), TWO_SEMS])
CORRELATE = call(
    correlate_kernel,
    (512, LANES),
    BF16,
    [VMEM] * 4,
    VMEM,
    [VMEM((2, BLK, LANES), F32)] * 6 + [VMEM((4, 64, LANES), F32), VMEM((LANES, LANES), F32)],
)
TOTAL = call(total_kernel, (512, LANES), BF16, [VMEM] * 2, VMEM)
UNPACK = call(unpack_kernel, (BLK, BLK), F32, [VMEM] * 2, HBM, [VMEM((BLK, BLK), F32), TWO_SEMS])


def on_device(inputs, out_grads):
    rows = PACK(*[pltpu.with_memory_space_constraint(a[0], HBM) for a in (inputs, out_grads)])
    rows = exchange(rows, PLANE_GROUPS)
    parts = CORRELATE(rows, one_hot(BLK, BLK, correlate_source), *make_tables())
    parts = exchange(parts, X_GROUPS)
    rows = TOTAL(parts, one_hot(512, LANES, total_source))
    rows = exchange(rows, PLANE_GROUPS)
    return UNPACK(rows, one_hot(BLK, BLK, unpack_source))


def solution(mesh):
    in_specs = (P("dp", "ctx", None), P("dp", "ctx", None))
    out_specs = P("ctx", None)
    return jax.shard_map(on_device, mesh=mesh, in_specs=in_specs, out_specs=out_specs, check_vma=False)
```

```python
import itertools
import math

import jax
import jax.numpy as jnp
import ml_dtypes
import numpy as np
from jax import lax
from jax.experimental import pallas as pl
from jax.experimental.pallas import tpu as pltpu
from jax.sharding import PartitionSpec as P

BLK = 256
NBLK = 32
LANES = 128
SIZES = {"x": 4, "y_lo": 2, "core": 2, "z": 8, "y_hi": 4}
F32 = jnp.float32
BF16 = jnp.bfloat16
LIMIT = 48 * 1024 * 1024


ORDER = {
    "x": (2, 0, 1, 3),
    "y_lo": (0, 1),
    "core": (1, 0),
    "z": (5, 6, 7, 0, 1, 2, 3, 4),
    "y_hi": (2, 3, 0, 1),
}


def groups_over(axes):
    rest = [a for a in SIZES if a not in axes]
    groups = []
    for fixed in itertools.product(*[range(SIZES[a]) for a in rest]):
        group = []
        for moving in itertools.product(*[ORDER[a] for a in axes]):
            place = dict(zip(rest, fixed)) | dict(zip(axes, moving))
            flat = 0
            for a in SIZES:
                flat = flat * SIZES[a] + place[a]
            group.append(flat)
        groups.append(group)
    return groups


SLOT = [0] * NBLK
for place, (z, y) in enumerate(itertools.product(ORDER["z"], ORDER["y_hi"])):
    SLOT[z * SIZES["y_hi"] + y] = place

PLANE_GROUPS = groups_over(("core", "z", "y_hi", "y_lo"))
X_GROUPS = groups_over(("x",))


def exchange(rows, groups):
    return lax.all_to_all(rows, ("dp", "ctx"), 0, 0, axis_index_groups=groups, tiled=True)


def make_tables():
    span = 2 * BLK
    freq = np.arange(BLK)[:, None]
    taps = np.arange(BLK)[None, :]
    angle = (freq * taps % span) * (2.0 * math.pi / span)
    signs = 1.0 - 2.0 * (taps % 2)
    sines = np.where(freq == 0, signs, np.sin(angle))
    forward = np.concatenate([np.cos(angle), sines], axis=0)
    weight = np.where(freq == 0, 1.0, 2.0) / span
    back = np.concatenate([weight * np.cos(angle), np.where(freq == 0, signs / span, -weight * np.sin(angle))], axis=0)
    return forward.T.astype(ml_dtypes.bfloat16), back.astype(ml_dtypes.bfloat16)


def dot(a, b):
    return jnp.dot(a, b, preferred_element_type=F32)


def permutation(source_of):
    row = lax.broadcasted_iota(jnp.int32, (BLK, BLK), 0)
    col = lax.broadcasted_iota(jnp.int32, (BLK, BLK), 1)
    return jnp.where(col == source_of(row), 1.0, 0.0).astype(BF16)


def one_hot(rows, cols, source_of):
    return (np.arange(cols)[None, :] == source_of(np.arange(rows))[:, None]).astype(ml_dtypes.bfloat16)


def pack_kernel(in_hbm, grad_hbm, out_ref, held, sems):
    copies = [pltpu.make_async_copy(ref, held.at[a], sems.at[a]) for a, ref in enumerate((in_hbm, grad_hbm))]
    for copy in copies:
        copy.start()
    perm = permutation(lambda m: (m & 7) * 32 + (m >> 3))
    turned = []
    for a in range(2):
        copies[a].wait()
        turned.append(jnp.transpose(held[a]))
    for part in range(4):
        pieces = []
        for a in range(2):
            for c in range(2):
                for th in range(2):
                    start = c * LANES + part * 32
                    pieces.append(turned[a][start : start + 32, th * LANES : (th + 1) * LANES])
        out_ref[part * BLK : (part + 1) * BLK, :] = dot(perm, jnp.concatenate(pieces, axis=0)).astype(BF16)


def correlate_source(m):
    a, th, j8, core, y, c = m >> 7, (m >> 6) & 1, (m >> 3) & 7, (m >> 2) & 1, (m >> 1) & 1, m & 1
    return core * 128 + (j8 * 2 + y) * 8 + a * 4 + c * 2 + th


def correlate_kernel(rows_ref, perm_ref, forward_ref, back_ref, out_ref, xa, xb, xc, ga, gb, gc, zed, ybuf):
    perm = perm_ref[...]
    blocks = [[], []]
    for part in range(4):
        both = [rows_ref[core * 512 + part * LANES : core * 512 + (part + 1) * LANES, :] for core in range(2)]
        q = dot(perm, jnp.concatenate(both, axis=0)).astype(BF16)
        for a in range(2):
            at = a * 128
            blocks[a].append(jnp.concatenate([q[at : at + 64], q[at + 64 : at + 128]], axis=1))
    first = lax.broadcasted_iota(jnp.int32, (BLK, LANES), 1) == 0
    forward = forward_ref[...]
    spec_in = dot(jnp.concatenate(blocks[0], axis=0), forward).astype(BF16).astype(F32)
    spec_grad = dot(jnp.concatenate(blocks[1], axis=0), forward).astype(BF16).astype(F32)
    for half in range(2):
        up = slice(half * LANES, (half + 1) * LANES)
        down = slice(BLK + half * LANES, BLK + (half + 1) * LANES)
        cos_in, sin_in = spec_in[:, up], spec_in[:, down]
        cos_grad, sin_grad = spec_grad[:, up], spec_grad[:, down]
        x_a, x_b, x_c = cos_in + sin_in, sin_in, cos_in
        g_a, g_b, g_c = cos_grad, cos_grad - sin_grad, cos_grad + sin_grad
        if half == 0:
            x_a = jnp.where(first, 0.0, x_a)
            x_b = jnp.where(first, -cos_in, x_b)
            x_c = jnp.where(first, -sin_in, x_c)
            g_b = jnp.where(first, cos_grad, g_b)
            g_c = jnp.where(first, sin_grad, g_c)
        for ref, value in ((xa, x_a), (xb, x_b), (xc, x_c), (ga, g_a), (gb, g_b), (gc, g_c)):
            ref[half] = value

    sign = jnp.where(lax.broadcasted_iota(jnp.int32, (8, LANES), 1) % 2 == 0, 1.0, -1.0)
    width = 4

    for half in range(2):
        def at(ref, j):
            return ref[half, SLOT[j] * 8 : (SLOT[j] + 1) * 8, :]

        after = [jnp.zeros((8, LANES), F32)] * 2
        for k0 in reversed(range(0, NBLK, width)):
            sums = [[None] * width for _ in range(3)]
            for i in range(k0, NBLK):
                grads = [at(ref, i) for ref in (ga, gb, gc)]
                for kk in range(width):
                    j = i - k0 - kk
                    if j < 0:
                        continue
                    for n, ref in enumerate((xa, xb, xc)):
                        product = grads[n] * at(ref, j)
                        sums[n][kk] = product if sums[n][kk] is None else sums[n][kk] + product
            for kk in reversed(range(width)):
                k = k0 + kk
                now = [sums[0][kk] - sums[1][kk], sums[0][kk] - sums[2][kk]]
                for part in range(2):
                    total = now[part] + sign * after[part]
                    total = total + pltpu.roll(total, 4, 0)
                    total = total + pltpu.roll(total, 2, 0)
                    zed[part * 2 + half, 2 * SLOT[k] : 2 * SLOT[k] + 2, :] = total[0:2]
                after = now
    z = jnp.concatenate([zed[n] for n in range(4)], axis=1)
    y = dot(z.astype(BF16), back_ref[...])
    for lh in range(2):
        ybuf[pl.ds(lh, 64, stride=2), :] = y[:, lh * LANES : (lh + 1) * LANES]
    y = ybuf[...].astype(BF16)
    for x in range(4):
        out_ref[x * LANES : (x + 1) * LANES, :] = y


def total_source(m):
    return ((m >> 3) & 31) * 4 + (m & 3)


def total_kernel(parts_ref, repeat_ref, out_ref):
    total = parts_ref[0:LANES].astype(F32)
    for n in range(1, 4):
        total = total + parts_ref[n * LANES : (n + 1) * LANES].astype(F32)
    out_ref[...] = dot(repeat_ref[...], total.astype(BF16)).astype(BF16)


def unpack_source(m):
    return (m & 127) * 4 + ((m >> 7) & 1) * 2 + (m >> 8)


def unpack_kernel(rows_ref, pick_ref, out_hbm, held, sems):
    received = rows_ref[...]
    copies = []
    for lh in range(2):
        rows = slice(lh * LANES, (lh + 1) * LANES)
        pick = pick_ref[:, lh * BLK : (lh + 1) * BLK]
        held[rows, :] = lax.dot_general(received, pick, (((0,), (0,)), ((), ())), preferred_element_type=F32)
        copies.append(pltpu.make_async_copy(held.at[rows], out_hbm.at[rows], sems.at[lh]))
        copies[-1].start()
    for copy in copies:
        copy.wait()


def call(kernel, shape, dtype, ins, out, scratch=()):
    return pl.pallas_call(
        kernel,
        out_shape=jax.ShapeDtypeStruct(shape, dtype),
        in_specs=[pl.BlockSpec(memory_space=space) for space in ins],
        out_specs=pl.BlockSpec(memory_space=out),
        scratch_shapes=list(scratch),
        compiler_params=pltpu.CompilerParams(vmem_limit_bytes=LIMIT),
    )


VMEM, HBM = pltpu.VMEM, pltpu.HBM
TWO_SEMS = pltpu.SemaphoreType.DMA((2,))
PACK = call(pack_kernel, (1024, LANES), BF16, [HBM] * 2, VMEM, [VMEM((2, BLK, BLK), BF16), TWO_SEMS])
CORRELATE = call(
    correlate_kernel,
    (512, LANES),
    BF16,
    [VMEM] * 4,
    VMEM,
    [VMEM((2, BLK, LANES), F32)] * 6 + [VMEM((4, 64, LANES), F32), VMEM((LANES, LANES), F32)],
)
TOTAL = call(total_kernel, (512, LANES), BF16, [VMEM] * 2, VMEM)
UNPACK = call(unpack_kernel, (BLK, BLK), F32, [VMEM] * 2, HBM, [VMEM((BLK, BLK), F32), TWO_SEMS])


def on_device(inputs, out_grads):
    rows = PACK(*[pltpu.with_memory_space_constraint(a[0], HBM) for a in (inputs, out_grads)])
    rows = exchange(rows, PLANE_GROUPS)
    parts = CORRELATE(rows, one_hot(BLK, BLK, correlate_source), *make_tables())
    parts = exchange(parts, X_GROUPS)
    rows = TOTAL(parts, one_hot(512, LANES, total_source))
    rows = exchange(rows, PLANE_GROUPS)
    return UNPACK(rows, one_hot(512, 512, unpack_source).T)


def solution(mesh):
    in_specs = (P("dp", "ctx", None), P("dp", "ctx", None))
    out_specs = P("ctx", None)
    return jax.shard_map(on_device, mesh=mesh, in_specs=in_specs, out_specs=out_specs, check_vma=False)
```

```python
import itertools
import math

import jax
import jax.numpy as jnp
import ml_dtypes
import numpy as np
from jax import lax
from jax.experimental import pallas as pl
from jax.experimental.pallas import tpu as pltpu
from jax.sharding import PartitionSpec as P

BLK = 256
NBLK = 32
LANES = 128
SIZES = {"x": 4, "y_lo": 2, "core": 2, "z": 8, "y_hi": 4}
F32 = jnp.float32
BF16 = jnp.bfloat16
LIMIT = 48 * 1024 * 1024


ORDER = {
    "x": (2, 0, 1, 3),
    "y_lo": (0, 1),
    "core": (1, 0),
    "z": (6, 7, 0, 1, 2, 3, 4, 5),
    "y_hi": (2, 3, 0, 1),
}


def groups_over(axes):
    rest = [a for a in SIZES if a not in axes]
    groups = []
    for fixed in itertools.product(*[range(SIZES[a]) for a in rest]):
        group = []
        for moving in itertools.product(*[ORDER[a] for a in axes]):
            place = dict(zip(rest, fixed)) | dict(zip(axes, moving))
            flat = 0
            for a in SIZES:
                flat = flat * SIZES[a] + place[a]
            group.append(flat)
        groups.append(group)
    return groups


SLOT = [0] * NBLK
for place, (z, y) in enumerate(itertools.product(ORDER["z"], ORDER["y_hi"])):
    SLOT[z * SIZES["y_hi"] + y] = place

PLANE_GROUPS = groups_over(("core", "z", "y_hi", "y_lo"))
X_GROUPS = groups_over(("x",))


def exchange(rows, groups):
    return lax.all_to_all(rows, ("dp", "ctx"), 0, 0, axis_index_groups=groups, tiled=True)


def make_tables():
    span = 2 * BLK
    freq = np.arange(BLK)[:, None]
    taps = np.arange(BLK)[None, :]
    angle = (freq * taps % span) * (2.0 * math.pi / span)
    signs = 1.0 - 2.0 * (taps % 2)
    sines = np.where(freq == 0, signs, np.sin(angle))
    forward = np.concatenate([np.cos(angle), sines], axis=0)
    weight = np.where(freq == 0, 1.0, 2.0) / span
    back = np.concatenate([weight * np.cos(angle), np.where(freq == 0, signs / span, -weight * np.sin(angle))], axis=0)
    return forward.T.astype(ml_dtypes.bfloat16), back.astype(ml_dtypes.bfloat16)


def dot(a, b):
    return jnp.dot(a, b, preferred_element_type=F32)


def permutation(source_of):
    row = lax.broadcasted_iota(jnp.int32, (BLK, BLK), 0)
    col = lax.broadcasted_iota(jnp.int32, (BLK, BLK), 1)
    return jnp.where(col == source_of(row), 1.0, 0.0).astype(BF16)


def one_hot(rows, cols, source_of):
    return (np.arange(cols)[None, :] == source_of(np.arange(rows))[:, None]).astype(ml_dtypes.bfloat16)


def pack_kernel(in_hbm, grad_hbm, out_ref, held, sems):
    copies = [pltpu.make_async_copy(ref, held.at[a], sems.at[a]) for a, ref in enumerate((in_hbm, grad_hbm))]
    for copy in copies:
        copy.start()
    perm = permutation(lambda m: (m & 7) * 32 + (m >> 3))
    turned = []
    for a in range(2):
        copies[a].wait()
        turned.append(jnp.transpose(held[a]))
    for part in range(4):
        pieces = []
        for a in range(2):
            for c in range(2):
                for th in range(2):
                    start = c * LANES + part * 32
                    pieces.append(turned[a][start : start + 32, th * LANES : (th + 1) * LANES])
        out_ref[part * BLK : (part + 1) * BLK, :] = dot(perm, jnp.concatenate(pieces, axis=0)).astype(BF16)


def correlate_source(m):
    a, th, j8, core, y, c = m >> 7, (m >> 6) & 1, (m >> 3) & 7, (m >> 2) & 1, (m >> 1) & 1, m & 1
    return core * 128 + (j8 * 2 + y) * 8 + a * 4 + c * 2 + th


def correlate_kernel(rows_ref, perm_ref, forward_ref, back_ref, out_ref, xa, xb, xc, ga, gb, gc, zed, ybuf):
    perm = perm_ref[...]
    blocks = [[], []]
    for part in range(4):
        both = [rows_ref[core * 512 + part * LANES : core * 512 + (part + 1) * LANES, :] for core in range(2)]
        q = dot(perm, jnp.concatenate(both, axis=0)).astype(BF16)
        for a in range(2):
            at = a * 128
            blocks[a].append(jnp.concatenate([q[at : at + 64], q[at + 64 : at + 128]], axis=1))
    first = lax.broadcasted_iota(jnp.int32, (BLK, LANES), 1) == 0
    forward = forward_ref[...]
    spec_in = dot(jnp.concatenate(blocks[0], axis=0), forward).astype(BF16).astype(F32)
    spec_grad = dot(jnp.concatenate(blocks[1], axis=0), forward).astype(BF16).astype(F32)
    for half in range(2):
        up = slice(half * LANES, (half + 1) * LANES)
        down = slice(BLK + half * LANES, BLK + (half + 1) * LANES)
        cos_in, sin_in = spec_in[:, up], spec_in[:, down]
        cos_grad, sin_grad = spec_grad[:, up], spec_grad[:, down]
        x_a, x_b, x_c = cos_in + sin_in, sin_in, cos_in
        g_a, g_b, g_c = cos_grad, cos_grad - sin_grad, cos_grad + sin_grad
        if half == 0:
            x_a = jnp.where(first, 0.0, x_a)
            x_b = jnp.where(first, -cos_in, x_b)
            x_c = jnp.where(first, -sin_in, x_c)
            g_b = jnp.where(first, cos_grad, g_b)
            g_c = jnp.where(first, sin_grad, g_c)
        for ref, value in ((xa, x_a), (xb, x_b), (xc, x_c), (ga, g_a), (gb, g_b), (gc, g_c)):
            ref[half] = value

    sign = jnp.where(lax.broadcasted_iota(jnp.int32, (8, LANES), 1) % 2 == 0, 1.0, -1.0)
    width = 4

    for half in range(2):
        def at(ref, j):
            return ref[half, SLOT[j] * 8 : (SLOT[j] + 1) * 8, :]

        after = [jnp.zeros((8, LANES), F32)] * 2
        for k0 in reversed(range(0, NBLK, width)):
            sums = [[None] * width for _ in range(3)]
            for i in range(k0, NBLK):
                grads = [at(ref, i) for ref in (ga, gb, gc)]
                for kk in range(width):
                    j = i - k0 - kk
                    if j < 0:
                        continue
                    for n, ref in enumerate((xa, xb, xc)):
                        product = grads[n] * at(ref, j)
                        sums[n][kk] = product if sums[n][kk] is None else sums[n][kk] + product
            for kk in reversed(range(width)):
                k = k0 + kk
                now = [sums[0][kk] - sums[1][kk], sums[0][kk] - sums[2][kk]]
                for part in range(2):
                    total = now[part] + sign * after[part]
                    total = total + pltpu.roll(total, 4, 0)
                    total = total + pltpu.roll(total, 2, 0)
                    zed[part * 2 + half, 2 * SLOT[k] : 2 * SLOT[k] + 2, :] = total[0:2]
                after = now
    z = jnp.concatenate([zed[n] for n in range(4)], axis=1)
    y = dot(z.astype(BF16), back_ref[...])
    for lh in range(2):
        ybuf[pl.ds(lh, 64, stride=2), :] = y[:, lh * LANES : (lh + 1) * LANES]
    y = ybuf[...].astype(BF16)
    for x in range(4):
        out_ref[x * LANES : (x + 1) * LANES, :] = y


def total_source(m):
    return ((m >> 3) & 31) * 4 + (m & 3)


def total_kernel(parts_ref, repeat_ref, out_ref):
    total = parts_ref[0:LANES].astype(F32)
    for n in range(1, 4):
        total = total + parts_ref[n * LANES : (n + 1) * LANES].astype(F32)
    out_ref[...] = dot(repeat_ref[...], total.astype(BF16)).astype(BF16)


def unpack_source(m):
    return (m & 63) * 4 + (m >> 6)


def unpack_kernel(rows_ref, perm_ref, out_hbm, held, sems):
    perm = perm_ref[...]
    halves = [dot(perm, rows_ref[part * BLK : (part + 1) * BLK, :]) for part in range(2)]
    copies = []
    for lh in range(2):
        rows = slice(lh * LANES, (lh + 1) * LANES)
        for c in range(2):
            at = (c * 2 + lh) * 64
            block = jnp.concatenate([halves[part][at : at + 64] for part in range(2)], axis=0)
            held[rows, c * LANES : (c + 1) * LANES] = jnp.transpose(block)
        copies.append(pltpu.make_async_copy(held.at[rows], out_hbm.at[rows], sems.at[lh]))
        copies[-1].start()
    for copy in copies:
        copy.wait()


def call(kernel, shape, dtype, ins, out, scratch=()):
    return pl.pallas_call(
        kernel,
        out_shape=jax.ShapeDtypeStruct(shape, dtype),
        in_specs=[pl.BlockSpec(memory_space=space) for space in ins],
        out_specs=pl.BlockSpec(memory_space=out),
        scratch_shapes=list(scratch),
        compiler_params=pltpu.CompilerParams(vmem_limit_bytes=LIMIT),
    )


VMEM, HBM = pltpu.VMEM, pltpu.HBM
TWO_SEMS = pltpu.SemaphoreType.DMA((2,))
PACK = call(pack_kernel, (1024, LANES), BF16, [HBM] * 2, VMEM, [VMEM((2, BLK, BLK), BF16), TWO_SEMS])
CORRELATE = call(
    correlate_kernel,
    (512, LANES),
    BF16,
    [VMEM] * 4,
    VMEM,
    [VMEM((2, BLK, LANES), F32)] * 6 + [VMEM((4, 64, LANES), F32), VMEM((LANES, LANES), F32)],
)
TOTAL = call(total_kernel, (512, LANES), BF16, [VMEM] * 2, VMEM)
UNPACK = call(unpack_kernel, (BLK, BLK), F32, [VMEM] * 2, HBM, [VMEM((BLK, BLK), F32), TWO_SEMS])


def on_device(inputs, out_grads):
    rows = PACK(*[pltpu.with_memory_space_constraint(a[0], HBM) for a in (inputs, out_grads)])
    rows = exchange(rows, PLANE_GROUPS)
    parts = CORRELATE(rows, one_hot(BLK, BLK, correlate_source), *make_tables())
    parts = exchange(parts, X_GROUPS)
    rows = TOTAL(parts, one_hot(512, LANES, total_source))
    rows = exchange(rows, PLANE_GROUPS)
    return UNPACK(rows, one_hot(BLK, BLK, unpack_source))


def solution(mesh):
    in_specs = (P("dp", "ctx", None), P("dp", "ctx", None))
    out_specs = P("ctx", None)
    return jax.shard_map(on_device, mesh=mesh, in_specs=in_specs, out_specs=out_specs, check_vma=False)
```
